32 devices in a mesh: groups: 2 (over y), ep: 8 (over z, core), hg: 2 (over x).
Axes of the slice: x: 2, y: 2, z: 4, core: 2. Of those that a mesh axis runs over, the one named last changes fastest.
Arguments:
- queries: bfloat16 [3, 128, 64, 128], P(None, ('groups', 'ep'), 'hg'), parts along dimension 1, may hold values from -12 to 12
- key_cache: bfloat16 [3, 128, 4, 96, 128], P(None, ('groups', 'ep'), 'hg'), parts along dimension 1, may hold values from -5 to 5
- value_cache: bfloat16 [3, 128, 4, 96, 128], P(None, ('groups', 'ep'), 'hg'), parts along dimension 1, may hold values from -6 to 6
- lengths: int32 [3, 128], P(None, ('groups', 'ep')), parts along dimension 1, may hold values from 2 to 96, as said below
- residual: bfloat16 [3, 128, 4096], P(None, ('groups', 'ep')), parts along dimension 1, may hold values from -6 to 6
- out_weight: bfloat16 [8192, 4096], P('hg', 'ep'), may hold values from -0.0625 to 0.0625
- norm_gain: float32 [4096], replicated, may hold values from 0.1 to 1.9
- routes: int32 [3, 128, 8], P(None, ('groups', 'ep')), parts along dimension 1, may hold values from 0 to 15, all different within a row; in each aligned block of 8 rows (0 to 7, 8 to 15, ..., all dimensions but the last counted through in order) at most 8 rows name the same one
- route_probs: float32 [3, 128, 8], P(None, ('groups', 'ep')), parts along dimension 1, may hold values from 0.05 to 1
- gate_weight: bfloat16 [16, 4096, 768], P('ep', None, 'hg'), may hold values from -0.09375 to 0.09375
- up_weight: bfloat16 [16, 4096, 768], P('ep', None, 'hg'), may hold values from -0.09375 to 0.09375
- down_weight: bfloat16 [16, 768, 4096], P('ep', 'hg'), may hold values from -0.21875 to 0.21875
Outputs:
- layer_out: bfloat16 [3, 128, 4096], P(None, ('groups', 'ep'), 'hg'), parts along dimension 1
The draws below stay inside these ranges and needn't reach their ends.
There are 2 independent parts, one for each index of `groups`. The reference program is written for one: setup_inputs(seed, part) draws one part's arguments, and reference() takes and returns one part's arrays. A program takes and returns all parts, laid end to end along the dimension named above; an argument that names none is the same for every part. Nothing has to cross between parts.
Inputs may be any that keep to these rules, and one draw needn't show every extreme that they name: `routes`: in the 8 rows of one micro-batch on one index of ep (aligned blocks), no expert is named more than 8 times, a bound that some block reaches; a row names 8 different experts. `lengths`: some row of every draw has all 96 slots live.
All inputs are finite; a program needn't handle non-finite values.
Results may differ from the reference program's by a relative error of at most 0.0075.
Values may be sent and summed in bfloat16 or wider, within the bound.
A program may use at most 128 MiB of HBM per device.

```python
import math
import jax
import jax.numpy as jnp
import numpy as np
from jax import lax

D = 4096
HEADS = 64
KV = 4
HD = 128
HID = 768
TOP = 8
L = 96
MB = 3
ROW_DEV = 8
EXPERTS = 16
ROWS = 64
CAP = 8
N_EP = 8


def draw_queries(key, part):
    key = jax.random.fold_in(key, 1)
    values = jnp.clip(jax.random.normal(key, (MB, ROWS, HEADS, HD), jnp.float32), -5.0, 5.0)
    return values.astype(jnp.bfloat16)


def draw_key_cache(key, part):
    key = jax.random.fold_in(key, 2)
    values = jnp.clip(jax.random.normal(key, (MB, ROWS, KV, L, HD), jnp.float32), -5.0, 5.0)
    return values.astype(jnp.bfloat16)


def draw_lengths(key, part):
    key = jax.random.fold_in(key, 3)
    drawn = jax.random.randint(key, (MB, ROWS), 2, L + 1)
    chosen = jax.random.randint(jax.random.fold_in(key, 4), (), 0, MB * ROWS)
    flat_index = lax.broadcasted_iota(jnp.int32, (MB, ROWS), 0) * ROWS + lax.broadcasted_iota(jnp.int32, (MB, ROWS), 1)
    return jnp.where(flat_index == chosen, L, drawn).astype(jnp.int32)


def block_scale(rng, extent, pieces, low, top_value):
    level, own = 1.0, jax.random.fold_in(rng, 6)
    for dim, shards_of in pieces:
        heights = jnp.exp(jax.random.uniform(jax.random.fold_in(own, dim), (shards_of,), jnp.float32, low / len(pieces), top_value / len(pieces)))
        level = level * jnp.repeat(heights, extent[dim] // shards_of).reshape([-1 if axis == dim else 1 for axis in range(len(extent))])
    return level


def deal_out(own_key, own, number, rows, number_of, top, limit, lean):
    sequence = jax.random.permutation(own_key, number_of)
    packed, ordinary = portions_of(number_of, rows * top, limit, lean, True), portions_of(number_of, rows * top, limit, lean, False)
    places = jnp.arange(number_of)

    def named(sizes, offset_by):
        used = int((sizes > 0).sum())
        fixed = max(1, used // 4)
        passed = fixed + (places - fixed + offset_by * (used - fixed)) % max(1, number_of - fixed)
        return jnp.zeros((number_of,), jnp.int32).at[sequence[jnp.where(places < fixed, places, passed)]].set(jnp.asarray(sizes, jnp.int32))

    sizes = jnp.where(number % 4 == 0, named(packed, number // 4), named(ordinary, number - number // 4 - 1))
    mixed = jax.random.permutation(jax.random.fold_in(own, 3), number_of)
    donor, receiver = mixed[0:number_of // 2 * 2:2], mixed[1:number_of // 2 * 2:2]
    margin = jnp.minimum(sizes[donor] - 1, limit - sizes[receiver]) // 2
    margin = jnp.where((donor == sequence[0]) | (receiver == sequence[0]) | (sizes[receiver] == 0), 0, jnp.maximum(margin, 0))
    passed = jax.random.randint(jax.random.fold_in(own, 4), (number_of // 2,), 0, 1 << 20) % (margin + 1)
    sizes = sizes.at[donor].add(-passed).at[receiver].add(passed)
    labels = jnp.searchsorted(jnp.cumsum(sizes), jnp.arange(rows * top), side="right").astype(jnp.int32)
    grid = labels.reshape(top, rows).T
    grid = grid[jax.random.permutation(jax.random.fold_in(own, 1), rows)]
    offset_by = jax.random.randint(jax.random.fold_in(own, 2), (rows, 1), 0, top)
    return jnp.take_along_axis(grid, (jnp.arange(top)[None, :] + offset_by) % top, axis=1)


def portions_of(count, total, limit, skew, full):
    loads = [(1 << 20) // math.isqrt(grade ** skew) + 1 for grade in range(1, count + 1)]
    largest = limit if full else min(limit, max(-(-total // count), total * loads[0] // sum(loads)))
    least = 1 if total - largest >= count - 1 else 0
    holding, spare = [largest] + [least] * (count - 1), total - largest - least * (count - 1)
    while spare > 0:
        free = [i for i in range(1, count) if holding[i] < largest] or [i for i in range(1, count) if holding[i] < limit]
        pool, left = sum([loads[i] for i in free]), spare
        for i in free:
            extra = min(limit - holding[i], max(1, left * loads[i] // pool), spare)
            holding[i] = holding[i] + extra
            spare = spare - extra
    return np.array(holding)


def bell_draw(own_key, dims, spread, limit, shards=(), held_as=jnp.bfloat16):
    array = spread * jax.random.normal(own_key, dims, jnp.float32)
    if shards:
        array = array * block_scale(own_key, dims, shards, -0.22, 0.18)
    return jnp.clip(array, -limit, limit).astype(held_as)


def setup_inputs(seed: int = 0, part: int = 0) -> dict:
    key_list = jax.random.split(jax.random.key(seed), 13)
    part_splits = jax.random.split(jax.random.fold_in(key_list[12], part), 13)
    queries = draw_queries(jax.random.fold_in(jax.random.fold_in(key_list[12], part), 71), part)
    key_cache = draw_key_cache(jax.random.fold_in(jax.random.fold_in(key_list[12], part), 71), part)
    value_cache = bell_draw(part_splits[2], (MB, ROWS, KV, L, HD), 1.0, 6.0, ((1, 8), (2, 2)))
    lengths = draw_lengths(jax.random.fold_in(jax.random.fold_in(key_list[12], part), 71), part)
    residual = bell_draw(part_splits[4], (MB, ROWS, D), 1.0, 6.0, ((1, 8),))
    out_weight = bell_draw(key_list[5], (HEADS * HD, D), (HEADS * HD) ** -0.5, 0.0625, ((0, 2), (1, 8)))
    norm_gain = jnp.clip(1.0 + 0.18 * jax.random.normal(key_list[6], (D,), jnp.float32), 0.1, 1.9)
    routes_keys = jax.random.split(jax.random.fold_in(part_splits[7], 1), MB * ROWS // ROW_DEV)
    routes_turns = jax.random.permutation(jax.random.fold_in(part_splits[7], 3), MB * ROWS // ROW_DEV)
    routes = jax.vmap(lambda own, number: deal_out(jax.random.fold_in(part_splits[7], 2), own, number, ROW_DEV, EXPERTS, TOP, CAP, 2))(routes_keys, routes_turns).reshape((MB, ROWS, TOP))
    route_probs = jnp.clip(jnp.exp(math.log(1.0) - 2.9957323 * jax.random.uniform(part_splits[8], (MB, ROWS, TOP), jnp.float32) ** block_scale(part_splits[8], (MB, ROWS, TOP), ((1, 8),), -0.2, 0.2)), 0.05, 1.0)
    gate_weight = bell_draw(key_list[9], (EXPERTS, D, HID), D ** -0.5, 0.09375, ((0, 8), (2, 2)))
    up_weight = bell_draw(key_list[10], (EXPERTS, D, HID), D ** -0.5, 0.09375, ((0, 8), (2, 2)))
    down_weight = bell_draw(key_list[11], (EXPERTS, HID, D), HID ** -0.5, 0.21875, ((0, 8), (1, 2)))
    return dict(queries=queries, key_cache=key_cache, value_cache=value_cache, lengths=lengths, residual=residual, out_weight=out_weight, norm_gain=norm_gain, routes=routes, route_probs=route_probs, gate_weight=gate_weight, up_weight=up_weight, down_weight=down_weight)


def attend_one(inputs):
    queries, key_cache, value_cache, lengths = inputs
    row_count = queries.shape[0]
    grouped = queries.astype(jnp.float32).reshape(row_count, KV, HEADS // KV, HD)
    scores = jnp.einsum('rgjd,rgtd->rgjt', grouped, key_cache.astype(jnp.float32)) / math.sqrt(HD)
    live_mask = jnp.arange(L, dtype=jnp.int32)[None, :] < lengths[:, None]
    scores = jnp.where(live_mask[:, None, None, :], scores, -1e+30)
    weights = jax.nn.softmax(scores, axis=-1).astype(jnp.bfloat16)
    mixed_heads = jnp.einsum('rgjt,rgtd->rgjd', weights.astype(jnp.float32), value_cache.astype(jnp.float32))
    return mixed_heads.astype(jnp.bfloat16).reshape(row_count, HEADS * HD)

def expert_apply(inputs):
    tokens, gate_matrix, up_matrix, down_matrix = inputs
    gate_value = jnp.dot(tokens, gate_matrix, preferred_element_type=jnp.float32)
    up_value = jnp.dot(tokens, up_matrix, preferred_element_type=jnp.float32)
    activation = (jax.nn.silu(gate_value) * up_value).astype(jnp.bfloat16)
    return jnp.dot(activation, down_matrix, preferred_element_type=jnp.float32).astype(jnp.bfloat16)

def reference(queries, key_cache, value_cache, lengths, residual, out_weight, norm_gain, routes, route_probs, gate_weight, up_weight, down_weight):
    attended = lax.map(attend_one, (queries, key_cache, value_cache, lengths))
    projected = jnp.dot(attended.reshape(MB * ROWS, HEADS * HD), out_weight, preferred_element_type=jnp.float32)
    hidden = residual.astype(jnp.float32) + projected.reshape(MB, ROWS, D)
    scale = lax.rsqrt(lax.optimization_barrier(jnp.mean(hidden * hidden, axis=-1, keepdims=True)) + 1e-06)
    payload = (hidden * scale * norm_gain).astype(jnp.bfloat16)
    gate_share = route_probs / lax.optimization_barrier(jnp.sum(route_probs, axis=-1, keepdims=True))
    blocks = routes.reshape(MB * N_EP, ROW_DEV * TOP)
    onehot = (blocks[:, :, None] == jnp.arange(EXPERTS, dtype=jnp.int32)[None, None, :]).astype(jnp.int32)
    before = jnp.cumsum(onehot, axis=1) - onehot
    slot_index = lax.optimization_barrier(jnp.sum(before * onehot, axis=-1)).astype(jnp.int32)
    position = (jnp.arange(MB * N_EP, dtype=jnp.int32)[:, None] * CAP + slot_index).astype(jnp.int32)
    tokens = jnp.repeat(payload.reshape(MB * N_EP, ROW_DEV, D), TOP, axis=1)
    buffer = jnp.zeros((EXPERTS, MB * N_EP * CAP, D), jnp.bfloat16).at[blocks, position].set(tokens)
    outputs = lax.map(expert_apply, (buffer, gate_weight, up_weight, down_weight))
    picked = outputs[blocks, position].reshape(MB, ROWS, TOP, D).astype(jnp.float32)
    expert_mix = lax.optimization_barrier(jnp.sum(gate_share[..., None] * picked, axis=2))
    return (hidden + expert_mix).astype(jnp.bfloat16)
```

```python
import functools
import math

import jax
import jax.numpy as jnp
from jax import lax
from jax.experimental import pallas as pl
from jax.experimental.pallas import tpu as pltpu
from jax.sharding import PartitionSpec as P

MESH = pl.DeviceIdType.MESH
F32 = jnp.float32
BF16 = jnp.bfloat16


def layer_kernel(
    dims,
    q_ref, k_ref, v_ref, len_ref, res_ref, gain_ref, routes_ref, probs_ref,
    wo_hbm, wg_hbm, wu_hbm, wd_hbm,
    out_ref,
    wo, wg, wu, wd, mixed, att, resb, wbuf, proj, hx_out, hx_in, hid,
    acc_g, acc_u, ssq, act, mine, d1_out, d1_in, d2_out, d2_in, d3_out, d3_in,
    w_sem, rs_send, rs_recv, sh_send, sh_recv, a_send, a_recv, hx_send, hx_recv,
    h_send, h_recv, d1_send, d1_recv, d2_send, d2_recv, d3_send, d3_recv,
):
    E, H, G, R, NC, NW, Q, QW, J = dims
    Z = E // 2
    ROWS = E * R
    D = res_ref.shape[1]
    CB = D // E
    DH = D // H
    me = lax.axis_index("ep")
    h = lax.axis_index("hg")
    z = me // 2
    c = me % 2
    partner = z * 2 + (1 - c)

    barrier = pltpu.get_barrier_semaphore()

    def greet_ep(i, _):
        pl.semaphore_signal(barrier, inc=1, device_id={"ep": (me + i) % E}, device_id_type=MESH)
        return 0

    def greet_hg(i, _):
        pl.semaphore_signal(barrier, inc=1, device_id={"hg": (h + i) % H}, device_id_type=MESH)
        return 0

    lax.fori_loop(1, E, greet_ep, 0)
    lax.fori_loop(1, H, greet_hg, 0)

    loads = [
        pltpu.make_async_copy(src, dst, w_sem.at[i])
        for i, (src, dst) in enumerate(((wo_hbm, wo), (wg_hbm, wg), (wu_hbm, wu), (wd_hbm, wd)))
    ]
    for load in loads:
        load.start()

    probs = probs_ref[...]
    share = probs / jnp.sum(probs, axis=-1, keepdims=True)
    routes = routes_ref[...]
    lanes = lax.broadcasted_iota(jnp.int32, (R, wbuf.shape[2]), 1)
    dense = jnp.zeros((R, wbuf.shape[2]), F32)
    for t in range(routes.shape[1]):
        dense = dense + jnp.where(lanes == routes[:, t : t + 1], share[:, t : t + 1], 0.0)
    wbuf[me] = dense

    pl.semaphore_wait(barrier, E - 1 + H - 1)

    def share_copy(dst):
        return pltpu.make_async_remote_copy(
            src_ref=wbuf.at[me], dst_ref=wbuf.at[me],
            send_sem=sh_send.at[dst], recv_sem=sh_recv.at[me],
            device_id={"ep": dst}, device_id_type=MESH,
        )

    def res_copy(dst):
        return pltpu.make_async_remote_copy(
            src_ref=res_ref.at[:, pl.ds(pl.multiple_of(dst * CB, CB), CB)], dst_ref=resb.at[me],
            send_sem=rs_send.at[dst], recv_sem=rs_recv.at[me],
            device_id={"ep": dst}, device_id_type=MESH,
        )

    def spread(i, _):
        dst = (me + i) % E
        res_copy(dst).start()
        share_copy(dst).start()
        return 0

    lax.fori_loop(1, E, spread, 0)
    resb[me] = res_ref[:, pl.ds(pl.multiple_of(me * CB, CB), CB)]

    def gather(place, send, recv, chunks, own_ready, process):
        def copy(k, block, way):
            target = (partner, me + 2, me - 2)[way]
            return pltpu.make_async_remote_copy(
                src_ref=place(k, block), dst_ref=place(k, block),
                send_sem=send.at[k, block, way], recv_sem=recv.at[k, block],
                device_id={"ep": target}, device_id_type=MESH,
            )

        def landed(k, block):
            pltpu.make_async_remote_copy(
                src_ref=place(k, block), dst_ref=place(k, block),
                send_sem=send.at[k, block, 0], recv_sem=recv.at[k, block],
                device_id={"ep": partner}, device_id_type=MESH,
            ).wait_recv()

        for k in range(chunks):
            own_ready(k)

            @pl.when(z < Z - 1)
            def _():
                copy(k, me, 1).start()

            @pl.when(z > 0)
            def _():
                copy(k, me, 2).start()

            copy(k, me, 0).start()

        def step(s, _):
            for k in range(chunks):

                @pl.when(z - s >= 0)
                def _():
                    block = me - 2 * s
                    landed(k, block)

                    @pl.when(z < Z - 1)
                    def _():
                        copy(k, block, 1).start()

                    copy(k, block, 0).start()

                @pl.when(z + s < Z)
                def _():
                    block = me + 2 * s
                    landed(k, block)

                    @pl.when(z > 0)
                    def _():
                        copy(k, block, 2).start()

                    copy(k, block, 0).start()

            before = s - 1

            @pl.when(z - before >= 0)
            def _():
                for k in range(chunks):
                    landed(k, partner - 2 * before)
                process(z - before)

            @pl.when((before > 0) & (z + before < Z))
            def _():
                for k in range(chunks):
                    landed(k, partner + 2 * before)
                process(z + before)

            return 0

        lax.fori_loop(1, Z + 1, step, 0)

        def drain(s, _):
            for k in range(chunks):

                @pl.when(z - s >= 0)
                def _():
                    block = me - 2 * s

                    @pl.when(z < Z - 1)
                    def _():
                        copy(k, block, 1).wait_send()

                    copy(k, block, 0).wait_send()

                    @pl.when((s == 0) & (z > 0))
                    def _():
                        copy(k, block, 2).wait_send()

                @pl.when((s > 0) & (z + s < Z))
                def _():
                    block = me + 2 * s

                    @pl.when(z > 0)
                    def _():
                        copy(k, block, 2).wait_send()

                    copy(k, block, 0).wait_send()

            return 0

        return lambda: lax.fori_loop(0, Z, drain, 0)

    heads = q_ref.shape[2]
    span = k_ref.shape[2]
    hd = q_ref.shape[3]

    def attend(g):
        scores = lax.dot_general(
            q_ref[:, g], k_ref[:, g], (((2,), (2,)), ((0,), (0,))), preferred_element_type=F32
        ) * (1.0 / math.sqrt(hd))
        slots = lax.broadcasted_iota(jnp.int32, (R, heads, span), 2)
        scores = jnp.where(slots < len_ref[...], scores, -1e30)
        top = jnp.max(scores, axis=-1, keepdims=True)
        weights = jnp.exp(scores - top)
        weights = (weights / jnp.sum(weights, axis=-1, keepdims=True)).astype(BF16)
        result = lax.dot_general(
            weights, v_ref[:, g], (((2,), (1,)), ((0,), (0,))), preferred_element_type=F32
        )
        mixed[...] = result.reshape(R * heads, hd)
        for j in range(heads):
            att[g, me, :, j * hd : (j + 1) * hd] = mixed[pl.ds(j, R, stride=heads), :].astype(BF16)

    drain_att = gather(
        lambda k, block: att.at[k, block], a_send, a_recv, G, attend, lambda chip: None
    )

    loads[0].wait()
    width = heads * hd

    def rows_of(ref_value):
        return ref_value.astype(F32).reshape(ROWS, ref_value.shape[-1]).astype(BF16)

    def hx_copy(k, i):
        return pltpu.make_async_remote_copy(
            src_ref=hx_out.at[k], dst_ref=hx_in.at[k, h],
            send_sem=hx_send.at[k, i], recv_sem=hx_recv.at[k, h],
            device_id={"hg": (h + i) % H}, device_id_type=MESH,
        )

    for k in range(NC):
        total = jnp.zeros((ROWS, NW), F32)
        for g in range(G):
            total = total + jnp.dot(
                rows_of(att[g]), wo[g * width : (g + 1) * width, k * NW : (k + 1) * NW],
                preferred_element_type=F32,
            )
        total = total.reshape(E, R, NW)
        hx_out[k] = total.astype(BF16)
        for i in range(1, H):
            hx_copy(k, i).start()
        proj[k] = total

    def res_landed(i, _):
        src = (me + i) % E
        pltpu.make_async_remote_copy(
            src_ref=resb.at[src], dst_ref=resb.at[src],
            send_sem=rs_send.at[src], recv_sem=rs_recv.at[src],
            device_id={"ep": src}, device_id_type=MESH,
        ).wait_recv()
        pltpu.make_async_remote_copy(
            src_ref=wbuf.at[src], dst_ref=wbuf.at[src],
            send_sem=sh_send.at[src], recv_sem=sh_recv.at[src],
            device_id={"ep": src}, device_id_type=MESH,
        ).wait_recv()
        return 0

    lax.fori_loop(1, E, res_landed, 0)

    def hidden_ready(k):
        value = proj[k] + resb[:, :, k * NW : (k + 1) * NW].astype(F32)
        for i in range(1, H):
            src = (h + i) % H
            pltpu.make_async_remote_copy(
                src_ref=hx_out.at[k], dst_ref=hx_in.at[k, src],
                send_sem=hx_send.at[k, i], recv_sem=hx_recv.at[k, src],
                device_id={"hg": src}, device_id_type=MESH,
            ).wait_recv()
            value = value + hx_in[k, src].astype(F32)
        hid[me * NC + k] = value.astype(BF16)

    acc_g[...] = jnp.zeros_like(acc_g)
    acc_u[...] = jnp.zeros_like(acc_u)
    ssq[...] = jnp.zeros_like(ssq)
    loads[1].wait()
    loads[2].wait()

    def experts_in(chip):
        def piece(i, _):
            p = chip * (2 * NC) + i
            start = pl.multiple_of(p * NW, NW)
            x = hid[p].astype(F32).reshape(ROWS, NW)
            ssq[...] += jnp.sum(x * x, axis=-1, keepdims=True)
            xb = (x * gain_ref[:, pl.ds(start, NW)]).astype(BF16)
            for j in range(J):
                acc_g[j] += jnp.dot(xb, wg[j, pl.ds(start, NW), :], preferred_element_type=F32)
                acc_u[j] += jnp.dot(xb, wu[j, pl.ds(start, NW), :], preferred_element_type=F32)
            return 0

        lax.fori_loop(0, 2 * NC, piece, 0)

    drain_hid = gather(
        lambda k, block: hid.at[block * NC + k], h_send, h_recv, NC, hidden_ready, experts_in
    )

    scale = lax.rsqrt(ssq[...] * (1.0 / D) + 1e-6)
    shares = wbuf[...].reshape(ROWS, wbuf.shape[2])
    lanes = lax.broadcasted_iota(jnp.int32, shares.shape, 1)
    for j in range(J):
        own = jnp.sum(jnp.where(lanes == me * J + j, shares, 0.0), axis=-1, keepdims=True)
        gate_value = acc_g[j] * scale
        up_value = acc_u[j] * (scale * own)
        act[j] = (gate_value * jax.nn.sigmoid(gate_value) * up_value).astype(BF16)

    loads[3].wait()

    def d1_copy(i, q):
        return pltpu.make_async_remote_copy(
            src_ref=d1_out.at[i, q], dst_ref=d1_in.at[i, q],
            send_sem=d1_send.at[i, q], recv_sem=d1_recv.at[i, q],
            device_id={"ep": partner}, device_id_type=MESH,
        )

    def d2_copy(i, q):
        return pltpu.make_async_remote_copy(
            src_ref=d2_out.at[i - 1, q], dst_ref=d2_in.at[i - 1, q],
            send_sem=d2_send.at[i - 1, q], recv_sem=d2_recv.at[i - 1, q],
            device_id={"hg": (h + i) % H}, device_id_type=MESH,
        )

    def d3_copy(i, q):
        there = (z + i) % Z
        return pltpu.make_async_remote_copy(
            src_ref=d3_out.at[q, there], dst_ref=d3_in.at[i - 1, q],
            send_sem=d3_send.at[i - 1, q], recv_sem=d3_recv.at[i - 1, q],
            device_id={"ep": there * 2 + c}, device_id_type=MESH,
        )

    def down(i, q):
        start = pl.multiple_of(((h + i) % H) * DH + q * QW, QW)
        total = jnp.zeros((ROWS, QW), F32)
        for j in range(J):
            total = total + jnp.dot(
                act[j], wd[j, :, pl.ds(start, QW)], preferred_element_type=F32
            )
        total = total.reshape(Z, 2, R, QW)
        first, second = total[:, 0], total[:, 1]
        d1_out[i, q] = jnp.where(c == 0, second, first).astype(BF16)
        d1_copy(i, q).start()
        mine[i, q] = jnp.where(c == 0, first, second)

    for q in range(Q):
        for i in range(1, H):
            down(i, q)
    for q in range(Q):
        down(0, q)
        for i in range(1, H):
            d1_copy(i, q).wait_recv()
            d2_out[i - 1, q] = (mine[i, q] + d1_in[i, q].astype(F32)).astype(BF16)
            d2_copy(i, q).start()

    for q in range(Q):
        d1_copy(0, q).wait_recv()
        total = mine[0, q] + d1_in[0, q].astype(F32)
        for i in range(1, H):
            d2_copy(i, q).wait_recv()
            total = total + d2_in[i - 1, q].astype(F32)
        mine[0, q] = total
        d3_out[q] = total.astype(BF16)
        for i in range(1, Z):
            d3_copy(i, q).start()

    per = QW // NW
    for q in range(Q):
        total = mine[0, q, z]
        for i in range(1, Z):
            d3_copy(i, q).wait_recv()
            total = total + d3_in[i - 1, q].astype(F32)
        for i in range(per):
            p = (h * DH + q * QW) // NW + i
            part = hid[p, me].astype(F32) + total[:, i * NW : (i + 1) * NW]
            out_ref[:, q * QW + i * NW : q * QW + (i + 1) * NW] = part.astype(BF16)

    drain_att()
    drain_hid()

    def spread_done(i, _):
        dst = (me + i) % E
        res_copy(dst).wait_send()
        share_copy(dst).wait_send()
        return 0

    lax.fori_loop(1, E, spread_done, 0)
    for k in range(NC):
        for i in range(1, H):
            hx_copy(k, i).wait_send()
    for q in range(Q):
        for i in range(H):
            d1_copy(i, q).wait_send()
        for i in range(1, H):
            d2_copy(i, q).wait_send()
        for i in range(1, Z):
            d3_copy(i, q).wait_send()


def shards(
    queries,
    key_cache,
    value_cache,
    lengths,
    residual,
    out_weight,
    norm_gain,
    routes,
    route_probs,
    gate_weight,
    up_weight,
    down_weight,
):
    E = lax.axis_size("ep")
    H = lax.axis_size("hg")
    batches, rows, heads, hd = queries.shape
    G, span = key_cache.shape[2], key_cache.shape[3]
    R = batches * rows
    D = residual.shape[2]
    J, _, hid_local = gate_weight.shape
    CB = D // E
    NC = 2 if CB % 256 == 0 else 1
    NW = CB // NC
    DH = D // H
    Q = max(1, DH // 512)
    QW = DH // Q
    Z = E // 2
    ROWS = E * R
    lane_count = -(-J * E // 128) * 128
    width = heads // G * hd
    dims = (E, H, G, R, NC, NW, Q, QW, J)
    vmem = pl.BlockSpec(memory_space=pltpu.VMEM)
    hbm = pl.BlockSpec(memory_space=pl.ANY)
    dma = pltpu.SemaphoreType.DMA
    out = pl.pallas_call(
        functools.partial(layer_kernel, dims),
        out_shape=jax.ShapeDtypeStruct((R, DH), BF16),
        in_specs=[vmem] * 8 + [hbm] * 4,
        out_specs=vmem,
        scratch_shapes=[
            pltpu.VMEM(out_weight.shape, BF16),
            pltpu.VMEM(gate_weight.shape, BF16),
            pltpu.VMEM(up_weight.shape, BF16),
            pltpu.VMEM(down_weight.shape, BF16),
            pltpu.VMEM((R * (heads // G), hd), F32),
            pltpu.VMEM((G, E, R, width), BF16),
            pltpu.VMEM((E, R, CB), BF16),
            pltpu.VMEM((E, R, lane_count), F32),
            pltpu.VMEM((NC, E, R, NW), F32),
            pltpu.VMEM((NC, E, R, NW), BF16),
            pltpu.VMEM((NC, H, E, R, NW), BF16),
            pltpu.VMEM((E * NC, E, R, NW), BF16),
            pltpu.VMEM((J, ROWS, hid_local), F32),
            pltpu.VMEM((J, ROWS, hid_local), F32),
            pltpu.VMEM((ROWS, 1), F32),
            pltpu.VMEM((J, ROWS, hid_local), BF16),
            pltpu.VMEM((H, Q, Z, R, QW), F32),
            pltpu.VMEM((H, Q, Z, R, QW), BF16),
            pltpu.VMEM((H, Q, Z, R, QW), BF16),
            pltpu.VMEM((H - 1, Q, Z, R, QW), BF16),
            pltpu.VMEM((H - 1, Q, Z, R, QW), BF16),
            pltpu.VMEM((Q, Z, R, QW), BF16),
            pltpu.VMEM((Z - 1, Q, R, QW), BF16),
            dma((4,)),
            dma((E,)), dma((E,)), dma((E,)), dma((E,)),
            dma((G, E, 3)), dma((G, E)),
            dma((NC, H)), dma((NC, H)),
            dma((NC, E, 3)), dma((NC, E)),
            dma((H, Q)), dma((H, Q)),
            dma((H - 1, Q)), dma((H - 1, Q)),
            dma((Z - 1, Q)), dma((Z - 1, Q)),
        ],
        compiler_params=pltpu.CompilerParams(
            collective_id=0, has_side_effects=True, vmem_limit_bytes=60 * 1024 * 1024
        ),
        name="layer",
    )(
        queries.reshape(R, G, heads // G, hd),
        key_cache.reshape(R, G, span, hd),
        value_cache.reshape(R, G, span, hd),
        lengths.reshape(R, 1, 1),
        residual.reshape(R, D),
        norm_gain.reshape(1, D),
        routes.reshape(R, routes.shape[2]),
        route_probs.reshape(R, route_probs.shape[2]),
        out_weight,
        gate_weight,
        up_weight,
        down_weight,
    )
    return out.reshape(batches, rows, DH)


def solution(mesh):
    return jax.shard_map(
        shards,
        mesh=mesh,
        in_specs=(
            P(None, ("groups", "ep"), "hg", None),
            P(None, ("groups", "ep"), "hg", None, None),
            P(None, ("groups", "ep"), "hg", None, None),
            P(None, ("groups", "ep")),
            P(None, ("groups", "ep"), None),
            P("hg", "ep"),
            P(),
            P(None, ("groups", "ep"), None),
            P(None, ("groups", "ep"), None),
            P("ep", None, "hg"),
            P("ep", None, "hg"),
            P("ep", "hg", None),
        ),
        out_specs=P(None, ("groups", "ep"), "hg"),
        check_vma=False,
    )
```

```python
import functools
import math

import jax
import jax.numpy as jnp
from jax import lax
from jax.experimental import pallas as pl
from jax.experimental.pallas import tpu as pltpu
from jax.sharding import PartitionSpec as P

MESH = pl.DeviceIdType.MESH
F32 = jnp.float32
BF16 = jnp.bfloat16


def layer_kernel(
    dims,
    len_ref, res_ref, gain_ref, routes_ref, probs_ref,
    q_hbm, k_hbm, v_hbm, wo_hbm, wg_hbm, wu_hbm, wd_hbm,
    out_ref,
    q_ref, k_ref, v_ref, wo, wg, wu, wd, mixed, att, resb, wbuf, hx_out, hx_in, hid,
    acc_g, acc_u, ssq, act, mine, d1_out, d1_in, d2_out, d2_in, d3_out, d3_in,
    w_sem, rs_send, rs_recv, sh_send, sh_recv, a_send, a_recv, hx_send, hx_recv,
    h_send, h_recv, d1_send, d1_recv, d2_send, d2_recv, d3_send, d3_recv,
):
    E, H, G, R, Q, QW, J, packed = dims
    Z = E // 2
    ROWS = E * R
    D = res_ref.shape[1]
    CB = D // E
    DH = D // H
    me = lax.axis_index("ep")
    h = lax.axis_index("hg")
    z = me // 2
    c = me % 2
    partner = z * 2 + (1 - c)
    PER = E // H

    def pos(e):
        return (e % H) * PER + e // H

    barrier = pltpu.get_barrier_semaphore()

    def greet_ep(i, _):
        pl.semaphore_signal(barrier, inc=1, device_id={"ep": (me + i) % E}, device_id_type=MESH)
        return 0

    def greet_hg(i, _):
        pl.semaphore_signal(barrier, inc=1, device_id={"hg": (h + i) % H}, device_id_type=MESH)
        return 0

    lax.fori_loop(1, E, greet_ep, 0)
    lax.fori_loop(1, H, greet_hg, 0)

    loads = [
        pltpu.make_async_copy(src, dst, w_sem.at[i])
        for i, (src, dst) in enumerate(((k_hbm, k_ref), (v_hbm, v_ref), (q_hbm, q_ref), (wo_hbm, wo), (wg_hbm, wg), (wu_hbm, wu), (wd_hbm, wd)))
    ]
    for load in loads:
        load.start()

    probs = probs_ref[...]
    share = probs / jnp.sum(probs, axis=-1, keepdims=True)
    routes = routes_ref[...]
    lanes = lax.broadcasted_iota(jnp.int32, (R, 128), 1)
    named = lanes % (E * J) if packed else lanes
    dense = jnp.zeros((R, 128), F32)
    for t in range(routes.shape[1]):
        dense = dense + jnp.where(named == routes[:, t : t + 1], share[:, t : t + 1], 0.0)
    if packed:
        row_in_eight = lax.broadcasted_iota(jnp.int32, (R, 128), 0) % 8
        dense = jnp.where(lanes // (E * J) == row_in_eight, dense, 0.0)
        dense = jnp.sum(dense.reshape(R // 8, 8, 128), axis=1)
    wbuf[pos(me)] = dense

    pl.semaphore_wait(barrier, E - 1 + H - 1)

    def share_copy(dst):
        return pltpu.make_async_remote_copy(
            src_ref=wbuf.at[pos(me)], dst_ref=wbuf.at[pos(me)],
            send_sem=sh_send.at[dst], recv_sem=sh_recv.at[me],
            device_id={"ep": dst}, device_id_type=MESH,
        )

    def res_copy(dst):
        return pltpu.make_async_remote_copy(
            src_ref=res_ref.at[:, pl.ds(pl.multiple_of(dst * CB, CB), CB)], dst_ref=resb.at[me // H],
            send_sem=rs_send.at[dst], recv_sem=rs_recv.at[me],
            device_id={"ep": dst}, device_id_type=MESH,
        )

    def spread(i, _):
        dst = (me + i) % E

        @pl.when(h == me % H)
        def _():
            res_copy(dst).start()

        share_copy(dst).start()
        return 0

    lax.fori_loop(1, E, spread, 0)

    @pl.when(h == me % H)
    def _():
        resb[me // H] = res_ref[:, pl.ds(pl.multiple_of(me * CB, CB), CB)]

    def gather(place, send, recv, chunks, own_ready, process):
        def copy(k, block, way):
            target = (partner, me + 2, me - 2)[way]
            return pltpu.make_async_remote_copy(
                src_ref=place(k, block), dst_ref=place(k, block),
                send_sem=send.at[k, block, way], recv_sem=recv.at[k, block],
                device_id={"ep": target}, device_id_type=MESH,
            )

        def landed(k, block):
            pltpu.make_async_remote_copy(
                src_ref=place(k, block), dst_ref=place(k, block),
                send_sem=send.at[k, block, 0], recv_sem=recv.at[k, block],
                device_id={"ep": partner}, device_id_type=MESH,
            ).wait_recv()

        for k in range(chunks):
            own_ready(k)

            @pl.when(z < Z - 1)
            def _():
                copy(k, me, 1).start()

            @pl.when(z > 0)
            def _():
                copy(k, me, 2).start()

            copy(k, me, 0).start()

        def step(s, _):
            for k in range(chunks):

                @pl.when(z - s >= 0)
                def _():
                    block = me - 2 * s
                    landed(k, block)

                    @pl.when(z < Z - 1)
                    def _():
                        copy(k, block, 1).start()

                    copy(k, block, 0).start()

                @pl.when(z + s < Z)
                def _():
                    block = me + 2 * s
                    landed(k, block)

                    @pl.when(z > 0)
                    def _():
                        copy(k, block, 2).start()

                    copy(k, block, 0).start()

            before = s - 1

            @pl.when(z - before >= 0)
            def _():
                for k in range(chunks):
                    landed(k, partner - 2 * before)
                process(z - before)

            @pl.when((before > 0) & (z + before < Z))
            def _():
                for k in range(chunks):
                    landed(k, partner + 2 * before)
                process(z + before)

            return 0

        lax.fori_loop(1, Z + 1, step, 0)

        def drain(s, _):
            for k in range(chunks):

                @pl.when(z - s >= 0)
                def _():
                    block = me - 2 * s

                    @pl.when(z < Z - 1)
                    def _():
                        copy(k, block, 1).wait_send()

                    copy(k, block, 0).wait_send()

                    @pl.when((s == 0) & (z > 0))
                    def _():
                        copy(k, block, 2).wait_send()

                @pl.when((s > 0) & (z + s < Z))
                def _():
                    block = me + 2 * s

                    @pl.when(z > 0)
                    def _():
                        copy(k, block, 2).wait_send()

                    copy(k, block, 0).wait_send()

            return 0

        return lambda: lax.fori_loop(0, Z, drain, 0)

    heads = q_ref.shape[2]
    span = k_ref.shape[2]
    hd = q_ref.shape[3]

    loads[0].wait()
    loads[1].wait()
    loads[2].wait()
    rows = R // len_ref.shape[0]
    live = jnp.stack(
        [jnp.full((heads, span), len_ref[r // rows, r % rows], jnp.int32) for r in range(R)]
    )

    def attend(g):
        scores = lax.dot_general(
            q_ref[:, g], k_ref[:, g], (((2,), (2,)), ((0,), (0,))), preferred_element_type=F32
        ) * (1.0 / math.sqrt(hd))
        slots = lax.broadcasted_iota(jnp.int32, (R, heads, span), 2)
        scores = jnp.where(slots < live, scores, -1e30)
        top = jnp.max(scores, axis=-1, keepdims=True)
        weights = jnp.exp(scores - top)
        weights = (weights / jnp.sum(weights, axis=-1, keepdims=True)).astype(BF16)
        result = lax.dot_general(
            weights, v_ref[:, g], (((2,), (1,)), ((0,), (0,))), preferred_element_type=F32
        )
        mixed[...] = result.reshape(R * heads, hd)
        for j in range(heads):
            att[g, pos(me), :, j * hd : (j + 1) * hd] = mixed[pl.ds(j, R, stride=heads), :].astype(BF16)

    drain_att = gather(
        lambda k, block: att.at[k, pos(block)], a_send, a_recv, G, attend, lambda chip: None
    )

    loads[3].wait()
    width = heads * hd

    def project(part):
        total = jnp.zeros((PER * R, CB), F32)
        for g in range(G):
            rows_in = att[g, pl.ds(part * PER, PER)].astype(F32).reshape(PER * R, width)
            total = total + jnp.dot(
                rows_in.astype(BF16), wo[g * width : (g + 1) * width, :],
                preferred_element_type=F32,
            )
        return total.reshape(PER, R, CB)

    def hx_copy(i):
        return pltpu.make_async_remote_copy(
            src_ref=hx_out.at[i - 1], dst_ref=hx_in.at[i - 1],
            send_sem=hx_send.at[i - 1], recv_sem=hx_recv.at[i - 1],
            device_id={"hg": (h + i) % H}, device_id_type=MESH,
        )

    for i in range(1, H):
        hx_out[i - 1] = project((h + i) % H).astype(BF16)
        hx_copy(i).start()
    own_part = project(h)

    def landed_at(ref, place, sem):
        pltpu.make_async_remote_copy(
            src_ref=ref.at[place], dst_ref=ref.at[place],
            send_sem=sem, recv_sem=sem,
            device_id={"ep": partner}, device_id_type=MESH,
        ).wait_recv()

    def spread_landed(i, _):
        src = (me + i) % E

        @pl.when(src % H == h)
        def _():
            landed_at(resb, src // H, rs_recv.at[src])

        landed_at(wbuf, pos(src), sh_recv.at[src])
        return 0

    lax.fori_loop(1, E, spread_landed, 0)
    own_part = own_part + resb[...].astype(F32)
    for i in range(1, H):
        hx_copy(i).wait_recv()
        own_part = own_part + hx_in[i - 1].astype(F32)
    hid[me, h] = own_part.astype(BF16)

    acc_g[...] = jnp.zeros_like(acc_g)
    acc_u[...] = jnp.zeros_like(acc_u)
    ssq[...] = jnp.zeros_like(ssq)
    loads[4].wait()
    loads[5].wait()

    def experts_in(chip):
        def piece(i, _):
            p = chip * 2 + i
            start = pl.multiple_of(p * CB, CB)
            x = hid[p].astype(F32).reshape(ROWS, CB)
            ssq[...] += jnp.sum(x * x, axis=-1, keepdims=True)
            xb = (x * gain_ref[:, pl.ds(start, CB)]).astype(BF16)
            for j in range(J):
                acc_g[j] += jnp.dot(xb, wg[j, pl.ds(start, CB), :], preferred_element_type=F32)
                acc_u[j] += jnp.dot(xb, wu[j, pl.ds(start, CB), :], preferred_element_type=F32)
            return 0

        lax.fori_loop(0, 2, piece, 0)

    def hid_copy(block, part, way):
        if way < 3:
            device = {"ep": (partner, me + 2, me - 2)[way]}
        else:
            device = {"hg": (h + way - 2) % H}
        return pltpu.make_async_remote_copy(
            src_ref=hid.at[block, part], dst_ref=hid.at[block, part],
            send_sem=h_send.at[block, part, way], recv_sem=h_recv.at[block, part],
            device_id=device, device_id_type=MESH,
        )

    def hid_pass(block, go, right, left):
        for way, wanted in ((1, right), (2, left)):
            if wanted is not False:

                @pl.when(wanted)
                def _():
                    go(hid_copy(block, h, way))

        for i in range(1, H):
            go(hid_copy(block, h, 2 + i))
        go(hid_copy(block, h, 0))

    def hid_cross(block, go, wait):
        for i in range(1, H):
            part = (h + i) % H
            if wait:
                hid_copy(block, part, 0).wait_recv()
            go(hid_copy(block, part, 0))

    def hid_take(chip):
        for part in range(H):
            hid_copy(chip * 2 + (1 - c), part, 0).wait_recv()
        experts_in(chip)

    def sides(s, action):
        @pl.when((s >= 0) & (z - s >= 0))
        def _():
            action(z - s, True)

        @pl.when((s > 0) & (z + s < Z))
        def _():
            action(z + s, False)

    def start(copy):
        copy.start()

    def sent(copy):
        copy.wait_send()

    hid_pass(me, start, z < Z - 1, z > 0)

    def hid_step(s, _):
        def forward(chip, from_left):
            block = chip * 2 + c
            hid_copy(block, h, 0).wait_recv()
            hid_pass(block, start, (z < Z - 1) if from_left else False, False if from_left else (z > 0))

        sides(s, forward)
        sides(s - 1, lambda chip, from_left: hid_cross(chip * 2 + c, start, True))
        sides(s - 2, lambda chip, from_left: hid_take(chip))
        return 0

    lax.fori_loop(1, Z + 2, hid_step, 0)

    def drain_hid():
        hid_pass(me, sent, z < Z - 1, z > 0)

        def drain(s, _):
            def passed(chip, from_left):
                hid_pass(
                    chip * 2 + c, sent, (z < Z - 1) if from_left else False, False if from_left else (z > 0)
                )

            @pl.when(s > 0)
            def _():
                sides(s, passed)

            sides(s, lambda chip, from_left: hid_cross(chip * 2 + c, sent, False))
            return 0

        lax.fori_loop(0, Z, drain, 0)

    scale = lax.rsqrt(ssq[...] * (1.0 / D) + 1e-6)
    shares = wbuf[...]
    if packed:
        shares = jnp.broadcast_to(
            shares.reshape(E * R // 8, 1, 128), (E * R // 8, 8, 128)
        )
    shares = shares.reshape(ROWS, 128)
    lanes = lax.broadcasted_iota(jnp.int32, (ROWS, 128), 1)
    offset = (lax.broadcasted_iota(jnp.int32, (ROWS, 128), 0) % 8) * (E * J) if packed else 0
    for j in range(J):
        own = jnp.sum(
            jnp.where(lanes == offset + (me * J + j), shares, 0.0), axis=-1, keepdims=True
        )
        gate_value = acc_g[j] * scale
        up_value = acc_u[j] * (scale * own)
        act[j] = (gate_value * jax.nn.sigmoid(gate_value) * up_value).astype(BF16)

    loads[6].wait()

    def d1_copy(i, q):
        return pltpu.make_async_remote_copy(
            src_ref=d1_out.at[i, q], dst_ref=d1_in.at[i, q],
            send_sem=d1_send.at[i, q], recv_sem=d1_recv.at[i, q],
            device_id={"ep": partner}, device_id_type=MESH,
        )

    def d2_copy(i, q):
        return pltpu.make_async_remote_copy(
            src_ref=d2_out.at[i - 1, q], dst_ref=d2_in.at[i - 1, q],
            send_sem=d2_send.at[i - 1, q], recv_sem=d2_recv.at[i - 1, q],
            device_id={"hg": (h + i) % H}, device_id_type=MESH,
        )

    def chip_place(chip):
        return (chip % (H // 2)) * PER + chip // (H // 2)

    def d3_copy(i, q):
        there = (z + i) % Z
        return pltpu.make_async_remote_copy(
            src_ref=d3_out.at[q, chip_place(there)], dst_ref=d3_in.at[i - 1, q],
            send_sem=d3_send.at[i - 1, q], recv_sem=d3_recv.at[i - 1, q],
            device_id={"ep": there * 2 + c}, device_id_type=MESH,
        )

    def down(i, q):
        start = pl.multiple_of(((h + i) % H) * DH + q * QW, QW)
        total = jnp.zeros((ROWS, QW), F32)
        for j in range(J):
            total = total + jnp.dot(
                act[j], wd[j, :, pl.ds(start, QW)], preferred_element_type=F32
            )
        total = total.reshape(H // 2, 2, PER, R, QW)
        first = total[:, 0].reshape(Z, R, QW)
        second = total[:, 1].reshape(Z, R, QW)
        d1_out[i, q] = jnp.where(c == 0, second, first).astype(BF16)
        d1_copy(i, q).start()
        mine[i, q] = jnp.where(c == 0, first, second)

    for q in range(Q):
        for i in range(1, H):
            down(i, q)
    for q in range(Q):
        down(0, q)
        for i in range(1, H):
            d1_copy(i, q).wait_recv()
            d2_out[i - 1, q] = (mine[i, q] + d1_in[i, q].astype(F32)).astype(BF16)
            d2_copy(i, q).start()

    for q in range(Q):
        d1_copy(0, q).wait_recv()
        total = mine[0, q] + d1_in[0, q].astype(F32)
        for i in range(1, H):
            d2_copy(i, q).wait_recv()
            total = total + d2_in[i - 1, q].astype(F32)
        mine[0, q] = total
        d3_out[q] = total.astype(BF16)
        for i in range(1, Z):
            d3_copy(i, q).start()

    part_width = min(CB, QW)
    for q in range(Q):
        total = mine[0, q, chip_place(z)]
        for i in range(1, Z):
            d3_copy(i, q).wait_recv()
            total = total + d3_in[i - 1, q].astype(F32)
        for i in range(QW // part_width):
            column = i * part_width
            p = (h * DH + q * QW + column) // CB
            part = hid[p, me % H, me // H].astype(F32) + total[:, column : column + part_width]
            out_ref[:, q * QW + column : q * QW + column + part_width] = part.astype(BF16)

    drain_att()
    drain_hid()

    def spread_done(i, _):
        dst = (me + i) % E

        @pl.when(h == me % H)
        def _():
            res_copy(dst).wait_send()

        share_copy(dst).wait_send()
        return 0

    lax.fori_loop(1, E, spread_done, 0)
    for i in range(1, H):
        hx_copy(i).wait_send()
    for q in range(Q):
        for i in range(H):
            d1_copy(i, q).wait_send()
        for i in range(1, H):
            d2_copy(i, q).wait_send()
        for i in range(1, Z):
            d3_copy(i, q).wait_send()


def shards(
    queries,
    key_cache,
    value_cache,
    lengths,
    residual,
    out_weight,
    norm_gain,
    routes,
    route_probs,
    gate_weight,
    up_weight,
    down_weight,
):
    E = lax.axis_size("ep")
    H = lax.axis_size("hg")
    batches, rows, heads, hd = queries.shape
    G, span = key_cache.shape[2], key_cache.shape[3]
    R = batches * rows
    D = residual.shape[2]
    J, _, hid_local = gate_weight.shape
    CB = D // E
    DH = D // H
    Q = max(1, DH // 512)
    QW = DH // Q
    PER = E // H
    packed = J * E * 8 == 128 and R % 8 == 0
    Z = E // 2
    ROWS = E * R
    share_rows = R // 8 if packed else R
    width = heads // G * hd
    dims = (E, H, G, R, Q, QW, J, packed)
    vmem = pl.BlockSpec(memory_space=pltpu.VMEM)
    hbm = pl.BlockSpec(memory_space=pl.ANY)
    dma = pltpu.SemaphoreType.DMA
    out = pl.pallas_call(
        functools.partial(layer_kernel, dims),
        out_shape=jax.ShapeDtypeStruct((R, DH), BF16),
        in_specs=[pl.BlockSpec(memory_space=pltpu.SMEM)] + [vmem] * 4 + [hbm] * 7,
        out_specs=vmem,
        scratch_shapes=[
            pltpu.VMEM((R, G, heads // G, hd), BF16),
            pltpu.VMEM((R, G, span, hd), BF16),
            pltpu.VMEM((R, G, span, hd), BF16),
            pltpu.VMEM(out_weight.shape, BF16),
            pltpu.VMEM(gate_weight.shape, BF16),
            pltpu.VMEM(up_weight.shape, BF16),
            pltpu.VMEM(down_weight.shape, BF16),
            pltpu.VMEM((R * (heads // G), hd), F32),
            pltpu.VMEM((G, E, R, width), BF16),
            pltpu.VMEM((PER, R, CB), BF16),
            pltpu.VMEM((E, share_rows, 128), F32),
            pltpu.VMEM((H - 1, PER, R, CB), BF16),
            pltpu.VMEM((H - 1, PER, R, CB), BF16),
            pltpu.VMEM((E, H, PER, R, CB), BF16),
            pltpu.VMEM((J, ROWS, hid_local), F32),
            pltpu.VMEM((J, ROWS, hid_local), F32),
            pltpu.VMEM((ROWS, 1), F32),
            pltpu.VMEM((J, ROWS, hid_local), BF16),
            pltpu.VMEM((H, Q, Z, R, QW), F32),
            pltpu.VMEM((H, Q, Z, R, QW), BF16),
            pltpu.VMEM((H, Q, Z, R, QW), BF16),
            pltpu.VMEM((H - 1, Q, Z, R, QW), BF16),
            pltpu.VMEM((H - 1, Q, Z, R, QW), BF16),
            pltpu.VMEM((Q, Z, R, QW), BF16),
            pltpu.VMEM((Z - 1, Q, R, QW), BF16),
            dma((7,)),
            dma((E,)), dma((E,)), dma((E,)), dma((E,)),
            dma((G, E, 3)), dma((G, E)),
            dma((H - 1,)), dma((H - 1,)),
            dma((E, H, H + 2)), dma((E, H)),
            dma((H, Q)), dma((H, Q)),
            dma((H - 1, Q)), dma((H - 1, Q)),
            dma((Z - 1, Q)), dma((Z - 1, Q)),
        ],
        compiler_params=pltpu.CompilerParams(
            collective_id=0, has_side_effects=True, vmem_limit_bytes=60 * 1024 * 1024
        ),
        name="layer",
    )(
        lengths,
        residual.reshape(R, D),
        norm_gain.reshape(1, D),
        routes.reshape(R, routes.shape[2]),
        route_probs.reshape(R, route_probs.shape[2]),
        queries.reshape(R, G, heads // G, hd),
        key_cache.reshape(R, G, span, hd),
        value_cache.reshape(R, G, span, hd),
        out_weight,
        gate_weight,
        up_weight,
        down_weight,
    )
    return out.reshape(batches, rows, DH)


def solution(mesh):
    return jax.shard_map(
        shards,
        mesh=mesh,
        in_specs=(
            P(None, ("groups", "ep"), "hg", None),
            P(None, ("groups", "ep"), "hg", None, None),
            P(None, ("groups", "ep"), "hg", None, None),
            P(None, ("groups", "ep")),
            P(None, ("groups", "ep"), None),
            P("hg", "ep"),
            P(),
            P(None, ("groups", "ep"), None),
            P(None, ("groups", "ep"), None),
            P("ep", None, "hg"),
            P("ep", None, "hg"),
            P("ep", "hg", None),
        ),
        out_specs=P(None, ("groups", "ep"), "hg"),
        check_vma=False,
    )
```

```python
import functools
import math

import jax
import jax.numpy as jnp
from jax import lax
from jax.experimental import pallas as pl
from jax.experimental.pallas import tpu as pltpu
from jax.sharding import PartitionSpec as P

MESH = pl.DeviceIdType.MESH
F32 = jnp.float32
BF16 = jnp.bfloat16


def layer_kernel(
    dims,
    len_ref, res_ref, gain_ref, routes_ref, probs_ref,
    q_hbm, k_hbm, v_hbm, wo_hbm, wg_hbm, wu_hbm, wd_hbm,
    out_ref,
    q_ref, k_ref, v_ref, wo, wg, wu, wd, mixed, att, resb, wbuf, hx_out, hx_in, hid,
    acc_g, acc_u, ssq, act, mine, d1_out, d1_in, d2_out, d2_in, d3_out, d3_in,
    w_sem, rs_send, rs_recv, sh_send, sh_recv, a_send, a_recv, hx_send, hx_recv,
    h_send, h_recv, d1_send, d1_recv, d2_send, d2_recv, d3_send, d3_recv,
):
    E, H, G, R, Q, QW, J, packed, SA, S = dims
    Z = E // 2
    ROWS = E * R
    D = res_ref.shape[1]
    CB = D // E
    DH = D // H
    me = lax.axis_index("ep")
    h = lax.axis_index("hg")
    z = me // 2
    c = me % 2
    partner = z * 2 + (1 - c)
    PER = E // H

    def pos(e):
        return (e % H) * PER + e // H

    barrier = pltpu.get_barrier_semaphore()

    def greet_ep(i, _):
        pl.semaphore_signal(barrier, inc=1, device_id={"ep": (me + i) % E}, device_id_type=MESH)
        return 0

    def greet_hg(i, _):
        pl.semaphore_signal(barrier, inc=1, device_id={"hg": (h + i) % H}, device_id_type=MESH)
        return 0

    lax.fori_loop(1, E, greet_ep, 0)
    lax.fori_loop(1, H, greet_hg, 0)

    loads = [
        pltpu.make_async_copy(src, dst, w_sem.at[i])
        for i, (src, dst) in enumerate(((k_hbm, k_ref), (v_hbm, v_ref), (q_hbm, q_ref), (wo_hbm, wo), (wg_hbm, wg), (wu_hbm, wu), (wd_hbm, wd)))
    ]
    for load in loads:
        load.start()

    probs = probs_ref[...]
    share = probs / jnp.sum(probs, axis=-1, keepdims=True)
    routes = routes_ref[...]
    lanes = lax.broadcasted_iota(jnp.int32, (R, 128), 1)
    named = lanes % (E * J) if packed else lanes
    dense = jnp.zeros((R, 128), F32)
    for t in range(routes.shape[1]):
        dense = dense + jnp.where(named == routes[:, t : t + 1], share[:, t : t + 1], 0.0)
    if packed:
        row_in_eight = lax.broadcasted_iota(jnp.int32, (R, 128), 0) % 8
        dense = jnp.where(lanes // (E * J) == row_in_eight, dense, 0.0)
        dense = jnp.sum(dense.reshape(R // 8, 8, 128), axis=1)
    wbuf[pos(me)] = dense

    heads = q_ref.shape[2]
    span = k_ref.shape[2]
    hd = q_ref.shape[3]

    loads[0].wait()
    loads[1].wait()
    loads[2].wait()
    rows = R // len_ref.shape[0]
    live = jnp.stack(
        [jnp.full((heads, span), len_ref[r // rows, r % rows], jnp.int32) for r in range(R)]
    )

    per_chunk = heads // SA

    def attend(g):
        scores = lax.dot_general(
            q_ref[:, g], k_ref[:, g], (((2,), (2,)), ((0,), (0,))), preferred_element_type=F32
        ) * (1.0 / math.sqrt(hd))
        slots = lax.broadcasted_iota(jnp.int32, (R, heads, span), 2)
        scores = jnp.where(slots < live, scores, -1e30)
        top = jnp.max(scores, axis=-1, keepdims=True)
        weights = jnp.exp(scores - top)
        weights = (weights / jnp.sum(weights, axis=-1, keepdims=True)).astype(BF16)
        result = lax.dot_general(
            weights, v_ref[:, g], (((2,), (1,)), ((0,), (0,))), preferred_element_type=F32
        )
        mixed[...] = result.reshape(R * heads, hd)
        for j in range(heads):
            chunk, column = g * SA + j // per_chunk, j % per_chunk * hd
            att[chunk, pos(me), :, column : column + hd] = mixed[pl.ds(j, R, stride=heads), :].astype(BF16)

    for g in range(G):
        attend(g)

    pl.semaphore_wait(barrier, E - 1 + H - 1)

    def share_copy(dst):
        return pltpu.make_async_remote_copy(
            src_ref=wbuf.at[pos(me)], dst_ref=wbuf.at[pos(me)],
            send_sem=sh_send.at[dst], recv_sem=sh_recv.at[me],
            device_id={"ep": dst}, device_id_type=MESH,
        )

    def res_copy(dst):
        return pltpu.make_async_remote_copy(
            src_ref=res_ref.at[:, pl.ds(pl.multiple_of(dst * CB, CB), CB)], dst_ref=resb.at[me // H],
            send_sem=rs_send.at[dst], recv_sem=rs_recv.at[me],
            device_id={"ep": dst}, device_id_type=MESH,
        )

    def spread(i, _):
        dst = (me + i) % E

        @pl.when(h == me % H)
        def _():
            res_copy(dst).start()

        share_copy(dst).start()
        return 0

    lax.fori_loop(1, E, spread, 0)

    @pl.when(h == me % H)
    def _():
        resb[me // H] = res_ref[:, pl.ds(pl.multiple_of(me * CB, CB), CB)]

    def gather(place, send, recv, chunks, process):
        def copy(k, block, way):
            target = (partner, me + 2, me - 2)[way]
            return pltpu.make_async_remote_copy(
                src_ref=place(k, block), dst_ref=place(k, block),
                send_sem=send.at[k, block, way], recv_sem=recv.at[k, block],
                device_id={"ep": target}, device_id_type=MESH,
            )

        def landed(k, block):
            pltpu.make_async_remote_copy(
                src_ref=place(k, block), dst_ref=place(k, block),
                send_sem=send.at[k, block, 0], recv_sem=recv.at[k, block],
                device_id={"ep": partner}, device_id_type=MESH,
            ).wait_recv()

        for k in range(chunks):

            @pl.when(z < Z - 1)
            def _():
                copy(k, me, 1).start()

            @pl.when(z > 0)
            def _():
                copy(k, me, 2).start()

            copy(k, me, 0).start()

        def step(s, _):
            for k in range(chunks):

                @pl.when(z - s >= 0)
                def _():
                    block = me - 2 * s
                    landed(k, block)

                    @pl.when(z < Z - 1)
                    def _():
                        copy(k, block, 1).start()

                    copy(k, block, 0).start()

                @pl.when(z + s < Z)
                def _():
                    block = me + 2 * s
                    landed(k, block)

                    @pl.when(z > 0)
                    def _():
                        copy(k, block, 2).start()

                    copy(k, block, 0).start()

            before = s - 1

            @pl.when(z - before >= 0)
            def _():
                for k in range(chunks):
                    landed(k, partner - 2 * before)
                process(z - before)

            @pl.when((before > 0) & (z + before < Z))
            def _():
                for k in range(chunks):
                    landed(k, partner + 2 * before)
                process(z + before)

            return 0

        lax.fori_loop(1, Z + 1, step, 0)

        def drain(s, _):
            for k in range(chunks):

                @pl.when(z - s >= 0)
                def _():
                    block = me - 2 * s

                    @pl.when(z < Z - 1)
                    def _():
                        copy(k, block, 1).wait_send()

                    copy(k, block, 0).wait_send()

                    @pl.when((s == 0) & (z > 0))
                    def _():
                        copy(k, block, 2).wait_send()

                @pl.when((s > 0) & (z + s < Z))
                def _():
                    block = me + 2 * s

                    @pl.when(z > 0)
                    def _():
                        copy(k, block, 2).wait_send()

                    copy(k, block, 0).wait_send()

            return 0

        return lambda: lax.fori_loop(0, Z, drain, 0)

    drain_att = gather(
        lambda k, block: att.at[k, pos(block)], a_send, a_recv, G * SA, lambda chip: None
    )

    loads[3].wait()
    width = per_chunk * hd

    def project(part):
        total = jnp.zeros((PER * R, CB), F32)
        for g in range(G * SA):
            rows_in = att[g, pl.ds(part * PER, PER)].astype(F32).reshape(PER * R, width)
            total = total + jnp.dot(
                rows_in.astype(BF16), wo[g * width : (g + 1) * width, :],
                preferred_element_type=F32,
            )
        return total.reshape(PER, R, CB)

    def piece_rows(u):
        return pl.ds(u * (PER // S), PER // S)

    def hx_copy(i, u):
        return pltpu.make_async_remote_copy(
            src_ref=hx_out.at[i - 1, piece_rows(u)], dst_ref=hx_in.at[i - 1, piece_rows(u)],
            send_sem=hx_send.at[i - 1, u], recv_sem=hx_recv.at[i - 1, u],
            device_id={"hg": (h + i) % H}, device_id_type=MESH,
        )

    for i in range(1, H):
        hx_out[i - 1] = project((h + i) % H).astype(BF16)
        for u in range(S):
            hx_copy(i, u).start()
    own_part = project(h)

    def landed_at(ref, place, sem):
        pltpu.make_async_remote_copy(
            src_ref=ref.at[place], dst_ref=ref.at[place],
            send_sem=sem, recv_sem=sem,
            device_id={"ep": partner}, device_id_type=MESH,
        ).wait_recv()

    def spread_landed(i, _):
        src = (me + i) % E

        @pl.when(src % H == h)
        def _():
            landed_at(resb, src // H, rs_recv.at[src])

        landed_at(wbuf, pos(src), sh_recv.at[src])
        return 0

    lax.fori_loop(1, E, spread_landed, 0)
    own_part = own_part + resb[...].astype(F32)

    def hidden_piece(u):
        first, last = u * (PER // S), (u + 1) * (PER // S)
        value = own_part[first:last]
        for i in range(1, H):
            hx_copy(i, u).wait_recv()
            value = value + hx_in[i - 1, first:last].astype(F32)
        hid[me, h, first:last] = value.astype(BF16)

    acc_g[...] = jnp.zeros_like(acc_g)
    acc_u[...] = jnp.zeros_like(acc_u)
    ssq[...] = jnp.zeros_like(ssq)
    loads[4].wait()
    loads[5].wait()

    def experts_in(chip):
        def piece(i, _):
            p = chip * 2 + i
            start = pl.multiple_of(p * CB, CB)
            x = hid[p].astype(F32).reshape(ROWS, CB)
            ssq[...] += jnp.sum(x * x, axis=-1, keepdims=True)
            xb = (x * gain_ref[:, pl.ds(start, CB)]).astype(BF16)
            for j in range(J):
                acc_g[j] += jnp.dot(xb, wg[j, pl.ds(start, CB), :], preferred_element_type=F32)
                acc_u[j] += jnp.dot(xb, wu[j, pl.ds(start, CB), :], preferred_element_type=F32)
            return 0

        lax.fori_loop(0, 2, piece, 0)

    def hid_copy(block, part, way, u):
        if way < 3:
            device = {"ep": (partner, me + 2, me - 2)[way]}
        else:
            device = {"hg": (h + way - 2) % H}
        return pltpu.make_async_remote_copy(
            src_ref=hid.at[block, part, piece_rows(u)],
            dst_ref=hid.at[block, part, piece_rows(u)],
            send_sem=h_send.at[block, part, u * (H + 2) + way],
            recv_sem=h_recv.at[block, part, u],
            device_id=device, device_id_type=MESH,
        )

    def hid_pass(block, u, go, right, left):
        for way, wanted in ((1, right), (2, left)):
            if wanted is not False:

                @pl.when(wanted)
                def _():
                    go(hid_copy(block, h, way, u))

        for i in range(1, H):
            go(hid_copy(block, h, 2 + i, u))
        go(hid_copy(block, h, 0, u))

    def hid_cross(block, u, go, wait):
        for i in range(1, H):
            part = (h + i) % H
            if wait:
                hid_copy(block, part, 0, u).wait_recv()
            go(hid_copy(block, part, 0, u))

    def hid_take(chip):
        for part in range(H):
            for u in range(S):
                hid_copy(chip * 2 + (1 - c), part, 0, u).wait_recv()
        experts_in(chip)

    def sides(s, action):
        @pl.when((s >= 0) & (z - s >= 0))
        def _():
            action(z - s, True)

        @pl.when((s > 0) & (z + s < Z))
        def _():
            action(z + s, False)

    def start(copy):
        copy.start()

    def sent(copy):
        copy.wait_send()

    for u in range(S):
        hidden_piece(u)
        hid_pass(me, u, start, z < Z - 1, z > 0)

    def hid_step(s, _):
        for u in range(S):

            def forward(chip, from_left):
                block = chip * 2 + c
                hid_copy(block, h, 0, u).wait_recv()
                hid_pass(
                    block, u, start,
                    (z < Z - 1) if from_left else False, False if from_left else (z > 0),
                )

            sides(s, forward)
        for u in range(S):
            sides(s - 1, lambda chip, from_left: hid_cross(chip * 2 + c, u, start, True))
        sides(s - 2, lambda chip, from_left: hid_take(chip))
        return 0

    lax.fori_loop(1, Z + 2, hid_step, 0)

    def drain_hid():
        for u in range(S):
            hid_pass(me, u, sent, z < Z - 1, z > 0)

        def drain(s, _):
            for u in range(S):

                def passed(chip, from_left):
                    hid_pass(
                        chip * 2 + c, u, sent,
                        (z < Z - 1) if from_left else False, False if from_left else (z > 0),
                    )

                @pl.when(s > 0)
                def _():
                    sides(s, passed)

                sides(s, lambda chip, from_left: hid_cross(chip * 2 + c, u, sent, False))
            return 0

        lax.fori_loop(0, Z, drain, 0)

    scale = lax.rsqrt(ssq[...] * (1.0 / D) + 1e-6)
    shares = wbuf[...]
    if packed:
        shares = jnp.broadcast_to(
            shares.reshape(E * R // 8, 1, 128), (E * R // 8, 8, 128)
        )
    shares = shares.reshape(ROWS, 128)
    lanes = lax.broadcasted_iota(jnp.int32, (ROWS, 128), 1)
    offset = (lax.broadcasted_iota(jnp.int32, (ROWS, 128), 0) % 8) * (E * J) if packed else 0
    for j in range(J):
        own = jnp.sum(
            jnp.where(lanes == offset + (me * J + j), shares, 0.0), axis=-1, keepdims=True
        )
        gate_value = acc_g[j] * scale
        up_value = acc_u[j] * (scale * own)
        act[j] = (gate_value * jax.nn.sigmoid(gate_value) * up_value).astype(BF16)

    loads[6].wait()

    def d1_copy(i, q):
        return pltpu.make_async_remote_copy(
            src_ref=d1_out.at[i, q], dst_ref=d1_in.at[i, q],
            send_sem=d1_send.at[i, q], recv_sem=d1_recv.at[i, q],
            device_id={"ep": partner}, device_id_type=MESH,
        )

    def d2_copy(i, q):
        return pltpu.make_async_remote_copy(
            src_ref=d2_out.at[i - 1, q], dst_ref=d2_in.at[i - 1, q],
            send_sem=d2_send.at[i - 1, q], recv_sem=d2_recv.at[i - 1, q],
            device_id={"hg": (h + i) % H}, device_id_type=MESH,
        )

    def chip_place(chip):
        return (chip % (H // 2)) * PER + chip // (H // 2)

    def d3_copy(i, q):
        there = (z + i) % Z
        return pltpu.make_async_remote_copy(
            src_ref=d3_out.at[q, chip_place(there)], dst_ref=d3_in.at[i - 1, q],
            send_sem=d3_send.at[i - 1, q], recv_sem=d3_recv.at[i - 1, q],
            device_id={"ep": there * 2 + c}, device_id_type=MESH,
        )

    def down(i, q):
        start = pl.multiple_of(((h + i) % H) * DH + q * QW, QW)
        total = jnp.zeros((ROWS, QW), F32)
        for j in range(J):
            total = total + jnp.dot(
                act[j], wd[j, :, pl.ds(start, QW)], preferred_element_type=F32
            )
        total = total.reshape(H // 2, 2, PER, R, QW)
        first = total[:, 0].reshape(Z, R, QW)
        second = total[:, 1].reshape(Z, R, QW)
        d1_out[i, q] = jnp.where(c == 0, second, first).astype(BF16)
        d1_copy(i, q).start()
        mine[i, q] = jnp.where(c == 0, first, second)

    for q in range(Q):
        for i in range(1, H):
            down(i, q)
    for q in range(Q):
        down(0, q)
        for i in range(1, H):
            d1_copy(i, q).wait_recv()
            d2_out[i - 1, q] = (mine[i, q] + d1_in[i, q].astype(F32)).astype(BF16)
            d2_copy(i, q).start()

    for q in range(Q):
        d1_copy(0, q).wait_recv()
        total = mine[0, q] + d1_in[0, q].astype(F32)
        for i in range(1, H):
            d2_copy(i, q).wait_recv()
            total = total + d2_in[i - 1, q].astype(F32)
        mine[0, q] = total
        d3_out[q] = total.astype(BF16)
        for i in range(1, Z):
            d3_copy(i, q).start()

    part_width = min(CB, QW)
    for q in range(Q):
        total = mine[0, q, chip_place(z)]
        for i in range(1, Z):
            d3_copy(i, q).wait_recv()
            total = total + d3_in[i - 1, q].astype(F32)
        for i in range(QW // part_width):
            column = i * part_width
            p = h * (DH // CB) + (q * QW + column) // CB
            inside = (q * QW + column) % CB
            part = hid[p, me % H, me // H, :, inside : inside + part_width].astype(F32)
            part = part + total[:, column : column + part_width]
            out_ref[:, q * QW + column : q * QW + column + part_width] = part.astype(BF16)

    drain_att()
    drain_hid()

    def spread_done(i, _):
        dst = (me + i) % E

        @pl.when(h == me % H)
        def _():
            res_copy(dst).wait_send()

        share_copy(dst).wait_send()
        return 0

    lax.fori_loop(1, E, spread_done, 0)
    for i in range(1, H):
        for u in range(S):
            hx_copy(i, u).wait_send()
    for q in range(Q):
        for i in range(H):
            d1_copy(i, q).wait_send()
        for i in range(1, H):
            d2_copy(i, q).wait_send()
        for i in range(1, Z):
            d3_copy(i, q).wait_send()


def shards(
    queries,
    key_cache,
    value_cache,
    lengths,
    residual,
    out_weight,
    norm_gain,
    routes,
    route_probs,
    gate_weight,
    up_weight,
    down_weight,
):
    E = lax.axis_size("ep")
    H = lax.axis_size("hg")
    batches, rows, heads, hd = queries.shape
    G, span = key_cache.shape[2], key_cache.shape[3]
    R = batches * rows
    D = residual.shape[2]
    J, _, hid_local = gate_weight.shape
    CB = D // E
    DH = D // H
    Q = max(1, DH // 256)
    QW = DH // Q
    PER = E // H
    packed = J * E * 8 == 128 and R % 8 == 0
    Z = E // 2
    ROWS = E * R
    share_rows = R // 8 if packed else R
    width = heads // G * hd
    SA = 2 if heads // G % 2 == 0 else 1
    S = 2 if PER % 2 == 0 else 1
    dims = (E, H, G, R, Q, QW, J, packed, SA, S)
    vmem = pl.BlockSpec(memory_space=pltpu.VMEM)
    hbm = pl.BlockSpec(memory_space=pl.ANY)
    dma = pltpu.SemaphoreType.DMA
    out = pl.pallas_call(
        functools.partial(layer_kernel, dims),
        out_shape=jax.ShapeDtypeStruct((R, DH), BF16),
        in_specs=[pl.BlockSpec(memory_space=pltpu.SMEM)] + [vmem] * 4 + [hbm] * 7,
        out_specs=vmem,
        scratch_shapes=[
            pltpu.VMEM((R, G, heads // G, hd), BF16),
            pltpu.VMEM((R, G, span, hd), BF16),
            pltpu.VMEM((R, G, span, hd), BF16),
            pltpu.VMEM(out_weight.shape, BF16),
            pltpu.VMEM(gate_weight.shape, BF16),
            pltpu.VMEM(up_weight.shape, BF16),
            pltpu.VMEM(down_weight.shape, BF16),
            pltpu.VMEM((R * (heads // G), hd), F32),
            pltpu.VMEM((G * SA, E, R, width // SA), BF16),
            pltpu.VMEM((PER, R, CB), BF16),
            pltpu.VMEM((E, share_rows, 128), F32),
            pltpu.VMEM((H - 1, PER, R, CB), BF16),
            pltpu.VMEM((H - 1, PER, R, CB), BF16),
            pltpu.VMEM((E, H, PER, R, CB), BF16),
            pltpu.VMEM((J, ROWS, hid_local), F32),
            pltpu.VMEM((J, ROWS, hid_local), F32),
            pltpu.VMEM((ROWS, 1), F32),
            pltpu.VMEM((J, ROWS, hid_local), BF16),
            pltpu.VMEM((H, Q, Z, R, QW), F32),
            pltpu.VMEM((H, Q, Z, R, QW), BF16),
            pltpu.VMEM((H, Q, Z, R, QW), BF16),
            pltpu.VMEM((H - 1, Q, Z, R, QW), BF16),
            pltpu.VMEM((H - 1, Q, Z, R, QW), BF16),
            pltpu.VMEM((Q, Z, R, QW), BF16),
            pltpu.VMEM((Z - 1, Q, R, QW), BF16),
            dma((7,)),
            dma((E,)), dma((E,)), dma((E,)), dma((E,)),
            dma((G * SA, E, 3)), dma((G * SA, E)),
            dma((H - 1, S)), dma((H - 1, S)),
            dma((E, H, S * (H + 2))), dma((E, H, S)),
            dma((H, Q)), dma((H, Q)),
            dma((H - 1, Q)), dma((H - 1, Q)),
            dma((Z - 1, Q)), dma((Z - 1, Q)),
        ],
        compiler_params=pltpu.CompilerParams(
            collective_id=0, has_side_effects=True, vmem_limit_bytes=60 * 1024 * 1024
        ),
        name="layer",
    )(
        lengths,
        residual.reshape(R, D),
        norm_gain.reshape(1, D),
        routes.reshape(R, routes.shape[2]),
        route_probs.reshape(R, route_probs.shape[2]),
        queries.reshape(R, G, heads // G, hd),
        key_cache.reshape(R, G, span, hd),
        value_cache.reshape(R, G, span, hd),
        out_weight,
        gate_weight,
        up_weight,
        down_weight,
    )
    return out.reshape(batches, rows, DH)


def solution(mesh):
    return jax.shard_map(
        shards,
        mesh=mesh,
        in_specs=(
            P(None, ("groups", "ep"), "hg", None),
            P(None, ("groups", "ep"), "hg", None, None),
            P(None, ("groups", "ep"), "hg", None, None),
            P(None, ("groups", "ep")),
            P(None, ("groups", "ep"), None),
            P("hg", "ep"),
            P(),
            P(None, ("groups", "ep"), None),
            P(None, ("groups", "ep"), None),
            P("ep", None, "hg"),
            P("ep", None, "hg"),
            P("ep", "hg", None),
        ),
        out_specs=P(None, ("groups", "ep"), "hg"),
        check_vma=False,
    )
```

```python
import functools
import math

import jax
import jax.numpy as jnp
from jax import lax
from jax.experimental import pallas as pl
from jax.experimental.pallas import tpu as pltpu
from jax.sharding import PartitionSpec as P

MESH = pl.DeviceIdType.MESH
F32 = jnp.float32
BF16 = jnp.bfloat16


def layer_kernel(
    dims,
    len_ref, res_ref, gain_ref, routes_ref, probs_ref,
    q_hbm, k_hbm, v_hbm, wo_hbm, wg_hbm, wu_hbm, wd_hbm,
    out_ref,
    q_ref, k_ref, v_ref, wo, wg, wu, wd, mixed, att, resb, wbuf, hx_out, hx_in, hid,
    acc_g, acc_u, ssq, act, mine, d1_out, d1_in, d2_out, d2_in, d3_out, d3_in,
    w_sem, rs_send, rs_recv, sh_send, sh_recv, a_send, a_recv, hx_send, hx_recv,
    h_send, h_recv, d1_send, d1_recv, d2_send, d2_recv, d3_send, d3_recv,
):
    E, H, G, R, Q, QW, J, packed, SA, S = dims
    Z = E // 2
    ROWS = E * R
    D = res_ref.shape[1]
    CB = D // E
    DH = D // H
    me = lax.axis_index("ep")
    h = lax.axis_index("hg")
    z = me // 2
    c = me % 2
    partner = z * 2 + (1 - c)
    PER = E // H

    def pos(e):
        return (e % H) * PER + e // H

    barrier = pltpu.get_barrier_semaphore()

    def greet_ep(i, _):
        pl.semaphore_signal(barrier, inc=1, device_id={"ep": (me + i) % E}, device_id_type=MESH)
        return 0

    def greet_hg(i, _):
        pl.semaphore_signal(barrier, inc=1, device_id={"hg": (h + i) % H}, device_id_type=MESH)
        return 0

    lax.fori_loop(1, E, greet_ep, 0)
    lax.fori_loop(1, H, greet_hg, 0)

    loads = [
        pltpu.make_async_copy(src, dst, w_sem.at[i])
        for i, (src, dst) in enumerate(((k_hbm, k_ref), (v_hbm, v_ref), (q_hbm, q_ref), (wo_hbm, wo), (wg_hbm, wg), (wu_hbm, wu), (wd_hbm, wd)))
    ]
    for load in loads:
        load.start()

    probs = probs_ref[...]
    share = probs / jnp.sum(probs, axis=-1, keepdims=True)
    routes = routes_ref[...]
    lanes = lax.broadcasted_iota(jnp.int32, (R, 128), 1)
    named = lanes % (E * J) if packed else lanes
    dense = jnp.zeros((R, 128), F32)
    for t in range(routes.shape[1]):
        dense = dense + jnp.where(named == routes[:, t : t + 1], share[:, t : t + 1], 0.0)
    if packed:
        row_in_eight = lax.broadcasted_iota(jnp.int32, (R, 128), 0) % 8
        dense = jnp.where(lanes // (E * J) == row_in_eight, dense, 0.0)
        dense = jnp.sum(dense.reshape(R // 8, 8, 128), axis=1)
    wbuf[pos(me)] = dense

    heads = q_ref.shape[2]
    span = k_ref.shape[2]
    hd = q_ref.shape[3]

    loads[0].wait()
    loads[1].wait()
    loads[2].wait()
    rows = R // len_ref.shape[0]
    live = jnp.stack(
        [jnp.full((heads, span), len_ref[r // rows, r % rows], jnp.int32) for r in range(R)]
    )

    per_chunk = heads // SA

    def attend(g):
        scores = lax.dot_general(
            q_ref[:, g], k_ref[:, g], (((2,), (2,)), ((0,), (0,))), preferred_element_type=F32
        ) * (1.0 / math.sqrt(hd))
        slots = lax.broadcasted_iota(jnp.int32, (R, heads, span), 2)
        scores = jnp.where(slots < live, scores, -1e30)
        top = jnp.max(scores, axis=-1, keepdims=True)
        weights = jnp.exp(scores - top)
        weights = (weights / jnp.sum(weights, axis=-1, keepdims=True)).astype(BF16)
        result = lax.dot_general(
            weights, v_ref[:, g], (((2,), (1,)), ((0,), (0,))), preferred_element_type=F32
        )
        mixed[...] = result.reshape(R * heads, hd)
        for j in range(heads):
            chunk, column = g * SA + j // per_chunk, j % per_chunk * hd
            att[chunk, pos(me), :, column : column + hd] = mixed[pl.ds(j, R, stride=heads), :].astype(BF16)

    for g in range(G):
        attend(g)

    pl.semaphore_wait(barrier, E - 1 + H - 1)

    def share_copy(dst):
        return pltpu.make_async_remote_copy(
            src_ref=wbuf.at[pos(me)], dst_ref=wbuf.at[pos(me)],
            send_sem=sh_send.at[dst], recv_sem=sh_recv.at[me],
            device_id={"ep": dst}, device_id_type=MESH,
        )

    def res_copy(dst):
        return pltpu.make_async_remote_copy(
            src_ref=res_ref.at[:, pl.ds(pl.multiple_of(dst * CB, CB), CB)], dst_ref=resb.at[me // H],
            send_sem=rs_send.at[dst], recv_sem=rs_recv.at[me],
            device_id={"ep": dst}, device_id_type=MESH,
        )

    def spread(i, _):
        dst = (me + i) % E

        @pl.when(h == me % H)
        def _():
            res_copy(dst).start()

        share_copy(dst).start()
        return 0

    lax.fori_loop(1, E, spread, 0)

    @pl.when(h == me % H)
    def _():
        resb[me // H] = res_ref[:, pl.ds(pl.multiple_of(me * CB, CB), CB)]

    def gather(place, send, recv, chunks, process):
        def copy(k, block, way):
            target = (partner, me + 2, me - 2)[way]
            return pltpu.make_async_remote_copy(
                src_ref=place(k, block), dst_ref=place(k, block),
                send_sem=send.at[k, block, way], recv_sem=recv.at[k, block],
                device_id={"ep": target}, device_id_type=MESH,
            )

        def landed(k, block):
            pltpu.make_async_remote_copy(
                src_ref=place(k, block), dst_ref=place(k, block),
                send_sem=send.at[k, block, 0], recv_sem=recv.at[k, block],
                device_id={"ep": partner}, device_id_type=MESH,
            ).wait_recv()

        for k in range(chunks):

            @pl.when(z < Z - 1)
            def _():
                copy(k, me, 1).start()

            @pl.when(z > 0)
            def _():
                copy(k, me, 2).start()

            copy(k, me, 0).start()

        def step(s, _):
            for k in range(chunks):

                @pl.when(z - s >= 0)
                def _():
                    block = me - 2 * s
                    landed(k, block)

                    @pl.when(z < Z - 1)
                    def _():
                        copy(k, block, 1).start()

                    copy(k, block, 0).start()

                @pl.when(z + s < Z)
                def _():
                    block = me + 2 * s
                    landed(k, block)

                    @pl.when(z > 0)
                    def _():
                        copy(k, block, 2).start()

                    copy(k, block, 0).start()

            before = s - 1

            @pl.when(z - before >= 0)
            def _():
                for k in range(chunks):
                    landed(k, partner - 2 * before)
                process(z - before)

            @pl.when((before > 0) & (z + before < Z))
            def _():
                for k in range(chunks):
                    landed(k, partner + 2 * before)
                process(z + before)

            return 0

        lax.fori_loop(1, Z + 1, step, 0)

        def drain(s, _):
            for k in range(chunks):

                @pl.when(z - s >= 0)
                def _():
                    block = me - 2 * s

                    @pl.when(z < Z - 1)
                    def _():
                        copy(k, block, 1).wait_send()

                    copy(k, block, 0).wait_send()

                    @pl.when((s == 0) & (z > 0))
                    def _():
                        copy(k, block, 2).wait_send()

                @pl.when((s > 0) & (z + s < Z))
                def _():
                    block = me + 2 * s

                    @pl.when(z > 0)
                    def _():
                        copy(k, block, 2).wait_send()

                    copy(k, block, 0).wait_send()

            return 0

        return lambda: lax.fori_loop(0, Z, drain, 0)

    drain_att = gather(
        lambda k, block: att.at[k, pos(block)], a_send, a_recv, G * SA, lambda chip: None
    )

    loads[3].wait()
    width = per_chunk * hd

    def project(part):
        total = jnp.zeros((PER * R, CB), F32)
        for g in range(G * SA):
            rows_in = att[g, pl.ds(part * PER, PER)].astype(F32).reshape(PER * R, width)
            total = total + jnp.dot(
                rows_in.astype(BF16), wo[g * width : (g + 1) * width, :],
                preferred_element_type=F32,
            )
        return total.reshape(PER, R, CB)

    def piece_rows(u):
        return pl.ds(u * (PER // S), PER // S)

    def hx_copy(i, u):
        return pltpu.make_async_remote_copy(
            src_ref=hx_out.at[i - 1, piece_rows(u)], dst_ref=hx_in.at[i - 1, piece_rows(u)],
            send_sem=hx_send.at[i - 1, u], recv_sem=hx_recv.at[i - 1, u],
            device_id={"hg": (h + i) % H}, device_id_type=MESH,
        )

    for i in range(1, H):
        hx_out[i - 1] = project((h + i) % H).astype(BF16)
        for u in range(S):
            hx_copy(i, u).start()
    own_part = project(h)

    def landed_at(ref, place, sem):
        pltpu.make_async_remote_copy(
            src_ref=ref.at[place], dst_ref=ref.at[place],
            send_sem=sem, recv_sem=sem,
            device_id={"ep": partner}, device_id_type=MESH,
        ).wait_recv()

    def spread_landed(i, _):
        src = (me + i) % E

        @pl.when(src % H == h)
        def _():
            landed_at(resb, src // H, rs_recv.at[src])

        landed_at(wbuf, pos(src), sh_recv.at[src])
        return 0

    lax.fori_loop(1, E, spread_landed, 0)
    own_part = own_part + resb[...].astype(F32)

    def hidden_piece(u):
        first, last = u * (PER // S), (u + 1) * (PER // S)
        value = own_part[first:last]
        for i in range(1, H):
            hx_copy(i, u).wait_recv()
            value = value + hx_in[i - 1, first:last].astype(F32)
        hid[me, h, first:last] = value.astype(BF16)

    acc_g[...] = jnp.zeros_like(acc_g)
    acc_u[...] = jnp.zeros_like(acc_u)
    ssq[...] = jnp.zeros_like(ssq)
    loads[4].wait()
    loads[5].wait()

    def experts_in(chip):
        def piece(i, _):
            p = chip * 2 + i
            start = pl.multiple_of(p * CB, CB)
            x = hid[p].astype(F32).reshape(ROWS, CB)
            ssq[...] += jnp.sum(x * x, axis=-1, keepdims=True)
            xb = (x * gain_ref[:, pl.ds(start, CB)]).astype(BF16)
            for j in range(J):
                acc_g[j] += jnp.dot(xb, wg[j, pl.ds(start, CB), :], preferred_element_type=F32)
                acc_u[j] += jnp.dot(xb, wu[j, pl.ds(start, CB), :], preferred_element_type=F32)
            return 0

        lax.fori_loop(0, 2, piece, 0)

    def hid_copy(block, part, way, u):
        if way < 3:
            device = {"ep": (partner, me + 2, me - 2)[way]}
        else:
            device = {"hg": (h + way - 2) % H}
        return pltpu.make_async_remote_copy(
            src_ref=hid.at[block, part, piece_rows(u)],
            dst_ref=hid.at[block, part, piece_rows(u)],
            send_sem=h_send.at[block, part, u * (H + 2) + way],
            recv_sem=h_recv.at[block, part, u],
            device_id=device, device_id_type=MESH,
        )

    def hid_pass(block, u, go, right, left):
        for way, wanted in ((1, right), (2, left)):
            if wanted is not False:

                @pl.when(wanted)
                def _():
                    go(hid_copy(block, h, way, u))

        for i in range(1, H):
            go(hid_copy(block, h, 2 + i, u))
        go(hid_copy(block, h, 0, u))

    def hid_cross(block, u, go, wait):
        for i in range(1, H):
            part = (h + i) % H
            if wait:
                hid_copy(block, part, 0, u).wait_recv()
            go(hid_copy(block, part, 0, u))

    def hid_take(chip):
        for part in range(H):
            for u in range(S):
                hid_copy(chip * 2 + (1 - c), part, 0, u).wait_recv()
        experts_in(chip)

    def sides(s, action):
        @pl.when((s >= 0) & (z - s >= 0))
        def _():
            action(z - s, True)

        @pl.when((s > 0) & (z + s < Z))
        def _():
            action(z + s, False)

    def start(copy):
        copy.start()

    def sent(copy):
        copy.wait_send()

    for u in range(S):
        hidden_piece(u)
        hid_pass(me, u, start, z < Z - 1, z > 0)

    def hid_step(s, _):
        for u in range(S):

            def forward(chip, from_left):
                block = chip * 2 + c
                hid_copy(block, h, 0, u).wait_recv()
                hid_pass(
                    block, u, start,
                    (z < Z - 1) if from_left else False, False if from_left else (z > 0),
                )

            sides(s, forward)
        for u in range(S):
            sides(s - 1, lambda chip, from_left: hid_cross(chip * 2 + c, u, start, True))
        sides(s - 2, lambda chip, from_left: hid_take(chip))
        return 0

    lax.fori_loop(1, Z + 2, hid_step, 0)

    def drain_hid():
        for u in range(S):
            hid_pass(me, u, sent, z < Z - 1, z > 0)

        def drain(s, _):
            for u in range(S):

                def passed(chip, from_left):
                    hid_pass(
                        chip * 2 + c, u, sent,
                        (z < Z - 1) if from_left else False, False if from_left else (z > 0),
                    )

                @pl.when(s > 0)
                def _():
                    sides(s, passed)

                sides(s, lambda chip, from_left: hid_cross(chip * 2 + c, u, sent, False))
            return 0

        lax.fori_loop(0, Z, drain, 0)

    scale = lax.rsqrt(ssq[...] * (1.0 / D) + 1e-6)
    shares = wbuf[...]
    if packed:
        shares = jnp.broadcast_to(
            shares.reshape(E * R // 8, 1, 128), (E * R // 8, 8, 128)
        )
    shares = shares.reshape(ROWS, 128)
    lanes = lax.broadcasted_iota(jnp.int32, (ROWS, 128), 1)
    offset = (lax.broadcasted_iota(jnp.int32, (ROWS, 128), 0) % 8) * (E * J) if packed else 0
    for j in range(J):
        own = jnp.sum(
            jnp.where(lanes == offset + (me * J + j), shares, 0.0), axis=-1, keepdims=True
        )
        gate_value = acc_g[j] * scale
        up_value = acc_u[j] * (scale * own)
        act[j] = (gate_value * jax.nn.sigmoid(gate_value) * up_value).astype(BF16)

    loads[6].wait()

    def d1_copy(i, q):
        return pltpu.make_async_remote_copy(
            src_ref=d1_out.at[i, q], dst_ref=d1_in.at[i, q],
            send_sem=d1_send.at[i, q], recv_sem=d1_recv.at[i, q],
            device_id={"ep": partner}, device_id_type=MESH,
        )

    def d2_copy(i, q):
        return pltpu.make_async_remote_copy(
            src_ref=d2_out.at[i - 1, q], dst_ref=d2_in.at[i - 1, q],
            send_sem=d2_send.at[i - 1, q], recv_sem=d2_recv.at[i - 1, q],
            device_id={"hg": (h + i) % H}, device_id_type=MESH,
        )

    def chip_place(chip):
        return (chip % (H // 2)) * PER + chip // (H // 2)

    def d3_copy(i, q):
        there = (z + i) % Z
        return pltpu.make_async_remote_copy(
            src_ref=d3_out.at[q, chip_place(there)], dst_ref=d3_in.at[i - 1, q],
            send_sem=d3_send.at[i - 1, q], recv_sem=d3_recv.at[i - 1, q],
            device_id={"ep": there * 2 + c}, device_id_type=MESH,
        )

    def down(i, q):
        start = pl.multiple_of(((h + i) % H) * DH + q * QW, QW)
        total = jnp.zeros((ROWS, QW), F32)
        for j in range(J):
            total = total + jnp.dot(
                act[j], wd[j, :, pl.ds(start, QW)], preferred_element_type=F32
            )
        total = total.reshape(H // 2, 2, PER, R, QW)
        first = total[:, 0].reshape(Z, R, QW)
        second = total[:, 1].reshape(Z, R, QW)
        d1_out[i, q] = jnp.where(c == 0, second, first).astype(BF16)
        d1_copy(i, q).start()
        mine[i, q] = jnp.where(c == 0, first, second)

    def cross(q):
        for i in range(1, H):
            d1_copy(i, q).wait_recv()
            d2_out[i - 1, q] = (mine[i, q] + d1_in[i, q].astype(F32)).astype(BF16)
            d2_copy(i, q).start()

    for q in range(Q):
        for i in range(1, H):
            down(i, q)
        down(0, q)
        if q > 0:
            cross(q - 1)
    cross(Q - 1)

    for q in range(Q):
        d1_copy(0, q).wait_recv()
        total = mine[0, q] + d1_in[0, q].astype(F32)
        for i in range(1, H):
            d2_copy(i, q).wait_recv()
            total = total + d2_in[i - 1, q].astype(F32)
        mine[0, q] = total
        d3_out[q] = total.astype(BF16)
        for i in range(1, Z):
            d3_copy(i, q).start()

    part_width = min(CB, QW)
    for q in range(Q):
        total = mine[0, q, chip_place(z)]
        for i in range(1, Z):
            d3_copy(i, q).wait_recv()
            total = total + d3_in[i - 1, q].astype(F32)
        for i in range(QW // part_width):
            column = i * part_width
            p = h * (DH // CB) + (q * QW + column) // CB
            inside = (q * QW + column) % CB
            part = hid[p, me % H, me // H, :, inside : inside + part_width].astype(F32)
            part = part + total[:, column : column + part_width]
            out_ref[:, q * QW + column : q * QW + column + part_width] = part.astype(BF16)

    drain_att()
    drain_hid()

    def spread_done(i, _):
        dst = (me + i) % E

        @pl.when(h == me % H)
        def _():
            res_copy(dst).wait_send()

        share_copy(dst).wait_send()
        return 0

    lax.fori_loop(1, E, spread_done, 0)
    for i in range(1, H):
        for u in range(S):
            hx_copy(i, u).wait_send()
    for q in range(Q):
        for i in range(H):
            d1_copy(i, q).wait_send()
        for i in range(1, H):
            d2_copy(i, q).wait_send()
        for i in range(1, Z):
            d3_copy(i, q).wait_send()


def shards(
    queries,
    key_cache,
    value_cache,
    lengths,
    residual,
    out_weight,
    norm_gain,
    routes,
    route_probs,
    gate_weight,
    up_weight,
    down_weight,
):
    E = lax.axis_size("ep")
    H = lax.axis_size("hg")
    batches, rows, heads, hd = queries.shape
    G, span = key_cache.shape[2], key_cache.shape[3]
    R = batches * rows
    D = residual.shape[2]
    J, _, hid_local = gate_weight.shape
    CB = D // E
    DH = D // H
    Q = max(1, DH // 512)
    QW = DH // Q
    PER = E // H
    packed = J * E * 8 == 128 and R % 8 == 0
    Z = E // 2
    ROWS = E * R
    share_rows = R // 8 if packed else R
    width = heads // G * hd
    SA = 2 if heads // G % 2 == 0 else 1
    S = 2 if PER % 2 == 0 else 1
    dims = (E, H, G, R, Q, QW, J, packed, SA, S)
    vmem = pl.BlockSpec(memory_space=pltpu.VMEM)
    hbm = pl.BlockSpec(memory_space=pl.ANY)
    dma = pltpu.SemaphoreType.DMA
    out = pl.pallas_call(
        functools.partial(layer_kernel, dims),
        out_shape=jax.ShapeDtypeStruct((R, DH), BF16),
        in_specs=[pl.BlockSpec(memory_space=pltpu.SMEM)] + [vmem] * 4 + [hbm] * 7,
        out_specs=vmem,
        scratch_shapes=[
            pltpu.VMEM((R, G, heads // G, hd), BF16),
            pltpu.VMEM((R, G, span, hd), BF16),
            pltpu.VMEM((R, G, span, hd), BF16),
            pltpu.VMEM(out_weight.shape, BF16),
            pltpu.VMEM(gate_weight.shape, BF16),
            pltpu.VMEM(up_weight.shape, BF16),
            pltpu.VMEM(down_weight.shape, BF16),
            pltpu.VMEM((R * (heads // G), hd), F32),
            pltpu.VMEM((G * SA, E, R, width // SA), BF16),
            pltpu.VMEM((PER, R, CB), BF16),
            pltpu.VMEM((E, share_rows, 128), F32),
            pltpu.VMEM((H - 1, PER, R, CB), BF16),
            pltpu.VMEM((H - 1, PER, R, CB), BF16),
            pltpu.VMEM((E, H, PER, R, CB), BF16),
            pltpu.VMEM((J, ROWS, hid_local), F32),
            pltpu.VMEM((J, ROWS, hid_local), F32),
            pltpu.VMEM((ROWS, 1), F32),
            pltpu.VMEM((J, ROWS, hid_local), BF16),
            pltpu.VMEM((H, Q, Z, R, QW), F32),
            pltpu.VMEM((H, Q, Z, R, QW), BF16),
            pltpu.VMEM((H, Q, Z, R, QW), BF16),
            pltpu.VMEM((H - 1, Q, Z, R, QW), BF16),
            pltpu.VMEM((H - 1, Q, Z, R, QW), BF16),
            pltpu.VMEM((Q, Z, R, QW), BF16),
            pltpu.VMEM((Z - 1, Q, R, QW), BF16),
            dma((7,)),
            dma((E,)), dma((E,)), dma((E,)), dma((E,)),
            dma((G * SA, E, 3)), dma((G * SA, E)),
            dma((H - 1, S)), dma((H - 1, S)),
            dma((E, H, S * (H + 2))), dma((E, H, S)),
            dma((H, Q)), dma((H, Q)),
            dma((H - 1, Q)), dma((H - 1, Q)),
            dma((Z - 1, Q)), dma((Z - 1, Q)),
        ],
        compiler_params=pltpu.CompilerParams(
            collective_id=0, has_side_effects=True, vmem_limit_bytes=60 * 1024 * 1024
        ),
        name="layer",
    )(
        lengths,
        residual.reshape(R, D),
        norm_gain.reshape(1, D),
        routes.reshape(R, routes.shape[2]),
        route_probs.reshape(R, route_probs.shape[2]),
        queries.reshape(R, G, heads // G, hd),
        key_cache.reshape(R, G, span, hd),
        value_cache.reshape(R, G, span, hd),
        out_weight,
        gate_weight,
        up_weight,
        down_weight,
    )
    return out.reshape(batches, rows, DH)


def solution(mesh):
    return jax.shard_map(
        shards,
        mesh=mesh,
        in_specs=(
            P(None, ("groups", "ep"), "hg", None),
            P(None, ("groups", "ep"), "hg", None, None),
            P(None, ("groups", "ep"), "hg", None, None),
            P(None, ("groups", "ep")),
            P(None, ("groups", "ep"), None),
            P("hg", "ep"),
            P(),
            P(None, ("groups", "ep"), None),
            P(None, ("groups", "ep"), None),
            P("ep", None, "hg"),
            P("ep", None, "hg"),
            P("ep", "hg", None),
        ),
        out_specs=P(None, ("groups", "ep"), "hg"),
        check_vma=False,
    )
```
